128 devices in a mesh: dp: 4 (over x), tensor: 4 (over y_hi, core), context: 8 (over y_lo, z).
Axes of the slice: x: 4, y: 4 (y_hi: 2, y_lo: 2; y = y_hi * 2 + y_lo), z: 4, core: 2. Of those that a mesh axis runs over, the one named last changes fastest.
Arguments:
- tokens: bfloat16 [16384, 4096], P(('dp', 'tensor', 'context')), may hold values from -6 to 6
- routes: int32 [16384, 2], P(('dp', 'tensor', 'context')), may hold values from 0 to 31, all different within a row; in each aligned block of 128 rows (0 to 127, 128 to 255, ...) at most 10 rows name the same one
- gates: float32 [16384, 2], P(('dp', 'tensor', 'context')), may hold values from 0.1 to 1
- cotangent: bfloat16 [16384, 4096], P(('dp', 'tensor', 'context')), may hold values from -3 to 3
- w_gate: bfloat16 [32, 4096, 768], P(('tensor', 'context'), 'dp'), may hold values from -0.09375 to 0.09375
- w_up: bfloat16 [32, 4096, 768], P(('tensor', 'context'), 'dp'), may hold values from -0.09375 to 0.09375
- w_down: bfloat16 [32, 768, 4096], P(('tensor', 'context'), None, 'dp'), may hold values from -0.21875 to 0.21875
Outputs:
- mixed: bfloat16 [16384, 4096], P(('dp', 'tensor', 'context'))
- d_tokens: bfloat16 [16384, 4096], P(('dp', 'tensor', 'context'))
- grad_gate: bfloat16 [32, 4096, 768], P(('tensor', 'context'), 'dp')
- grad_up: bfloat16 [32, 4096, 768], P(('tensor', 'context'), 'dp')
- grad_down: bfloat16 [32, 768, 4096], P(('tensor', 'context'), None, 'dp')
The draws below stay inside these ranges and needn't reach their ends.
Inputs may be any that keep to these rules, and one draw needn't show every extreme that they name: `routes`: each row names 2 different experts; within the rows of one device no expert is named more than 10 times, a bound that some block reaches.
All inputs are finite; a program needn't handle non-finite values.
Results may differ from the reference program's by a relative error of at most 0.023.
Values may be sent and summed in bfloat16 or wider, within the bound.
A program may use at most 128 MiB of HBM per device.

```python
import math
import jax
import jax.numpy as jnp
import numpy as np
from jax import lax

D = 4096
FF = 768
TOK_DEV = 128
TOP = 2
EXPERTS = 32
CAP = 10
TOKENS = 16384
N_DP = 4
N_TENSOR = 4
N_CONTEXT = 8


def block_levels(rng, dims, cuts, low, largest):
    level, own = 1.0, jax.random.fold_in(rng, 6)
    for position, parts in cuts:
        steps = jnp.exp(jax.random.uniform(jax.random.fold_in(own, position), (parts,), jnp.float32, low / len(cuts), largest / len(cuts)))
        level = level * jnp.repeat(steps, dims[position] // parts).reshape([-1 if axis == position else 1 for axis in range(len(dims))])
    return level


def deal_out(key, own, number, rows, amount, top, bound, skew):
    order = jax.random.permutation(key, amount)
    crowded, common = portions_of(amount, rows * top, bound, skew, True), portions_of(amount, rows * top, bound, skew, False)
    places = jnp.arange(amount)

    def named(tallies, rotation):
        used = int((tallies > 0).sum())
        fixed = max(1, used // 4)
        shifted = fixed + (places - fixed + rotation * (used - fixed)) % max(1, amount - fixed)
        return jnp.zeros((amount,), jnp.int32).at[order[jnp.where(places < fixed, places, shifted)]].set(jnp.asarray(tallies, jnp.int32))

    tallies = jnp.where(number % 4 == 0, named(crowded, number // 4), named(common, number - number // 4 - 1))
    mixed = jax.random.permutation(jax.random.fold_in(own, 3), amount)
    source_of, taker = mixed[0:amount // 2 * 2:2], mixed[1:amount // 2 * 2:2]
    margin = jnp.minimum(tallies[source_of] - 1, bound - tallies[taker]) // 2
    margin = jnp.where((source_of == order[0]) | (taker == order[0]) | (tallies[taker] == 0), 0, jnp.maximum(margin, 0))
    shifted = jax.random.randint(jax.random.fold_in(own, 4), (amount // 2,), 0, 1 << 20) % (margin + 1)
    tallies = tallies.at[source_of].add(-shifted).at[taker].add(shifted)
    members = jnp.searchsorted(jnp.cumsum(tallies), jnp.arange(rows * top), side="right").astype(jnp.int32)
    grid = members.reshape(top, rows).T
    grid = grid[jax.random.permutation(jax.random.fold_in(own, 1), rows)]
    rotation = jax.random.randint(jax.random.fold_in(own, 2), (rows, 1), 0, top)
    return jnp.take_along_axis(grid, (jnp.arange(top)[None, :] + rotation) % top, axis=1)


def portions_of(number_of, total, limit, lean, full):
    weights = [(1 << 20) // math.isqrt(rank ** lean) + 1 for rank in range(1, number_of + 1)]
    largest = limit if full else min(limit, max(-(-total // number_of), total * weights[0] // sum(weights)))
    least = 1 if total - largest >= number_of - 1 else 0
    given, spare = [largest] + [least] * (number_of - 1), total - largest - least * (number_of - 1)
    while spare > 0:
        movable = [i for i in range(1, number_of) if given[i] < largest] or [i for i in range(1, number_of) if given[i] < limit]
        pool, remaining = sum([weights[i] for i in movable]), spare
        for i in movable:
            more = min(limit - given[i], max(1, remaining * weights[i] // pool), spare)
            given[i] = given[i] + more
            spare = spare - more
    return np.array(given)


def noise(key, dims, deviation, reach, cuts=(), kind=jnp.bfloat16):
    values = deviation * jax.random.normal(key, dims, jnp.float32)
    if cuts:
        values = values * block_levels(key, dims, cuts, -0.22, 0.18)
    return jnp.clip(values, -reach, reach).astype(kind)


def setup_inputs(seed: int = 0) -> dict:
    splits = jax.random.split(jax.random.key(seed), 8)
    tokens = noise(splits[0], (TOKENS, D), 1.0, 6.0, ((0, 128),))
    routes_keys = jax.random.split(jax.random.fold_in(splits[1], 1), TOKENS // TOK_DEV)
    routes_turns = jax.random.permutation(jax.random.fold_in(splits[1], 3), TOKENS // TOK_DEV)
    routes = jax.vmap(lambda own, number: deal_out(jax.random.fold_in(splits[1], 2), own, number, TOK_DEV, EXPERTS, TOP, CAP, 2))(routes_keys, routes_turns).reshape((TOKENS, TOP))
    gates = jnp.clip(jnp.exp(math.log(1.0) - 2.3025851 * jax.random.uniform(splits[2], (TOKENS, TOP), jnp.float32) ** block_levels(splits[2], (TOKENS, TOP), ((0, 128),), -0.2, 0.2)), 0.1, 1.0)
    cotangent = noise(splits[3], (TOKENS, D), 0.5, 3.0, ((0, 128),))
    w_gate = noise(splits[4], (EXPERTS, D, FF), D ** -0.5, 0.09375, ((0, 32), (1, 4)))
    w_up = noise(splits[5], (EXPERTS, D, FF), D ** -0.5, 0.09375, ((0, 32), (1, 4)))
    w_down = noise(splits[6], (EXPERTS, FF, D), FF ** -0.5, 0.21875, ((0, 32), (2, 4)))
    return dict(tokens=tokens, routes=routes, gates=gates, cotangent=cotangent, w_gate=w_gate, w_up=w_up, w_down=w_down)


def slot_tables(routes, gates, experts, cap):
    tok, top = routes.shape
    pairs = tok * top
    flat_exp = routes.reshape(pairs)
    chosen = (flat_exp[:, None] == jnp.arange(experts, dtype=jnp.int32)[None, :]).astype(jnp.int32)
    before = jnp.cumsum(chosen, axis=0) - chosen
    slot = jnp.sum(before * chosen, axis=1)
    dest = (flat_exp * cap + slot).astype(jnp.int32)
    match = (dest[None, :] == jnp.arange(experts * cap, dtype=jnp.int32)[:, None]).astype(jnp.int32)
    filled = jnp.sum(match, axis=1)
    owner = (jnp.sum(match * jnp.arange(pairs, dtype=jnp.int32)[None, :], axis=1) // top).astype(jnp.int32)
    weight = jnp.sum(match.astype(jnp.float32) * gates.reshape(pairs)[None, :], axis=1)
    return dest, owner, filled, weight


def expert_pass(x_rows, dy_rows, w_gate, w_up, w_down):
    gate_h = jnp.dot(x_rows, w_gate, preferred_element_type=jnp.float32)
    up_h = jnp.dot(x_rows, w_up, preferred_element_type=jnp.float32)
    sigma = jax.nn.sigmoid(gate_h)
    active = gate_h * sigma
    hidden = (active * up_h).astype(jnp.bfloat16)
    y_rows = jnp.dot(hidden, w_down, preferred_element_type=jnp.float32).astype(jnp.bfloat16)
    d_hidden = jnp.dot(dy_rows, w_down.T, preferred_element_type=jnp.float32)
    d_gate = (d_hidden * up_h * sigma * (1.0 + gate_h * (1.0 - sigma))).astype(jnp.bfloat16)
    d_up = (d_hidden * active).astype(jnp.bfloat16)
    dx_rows = (jnp.dot(d_gate, w_gate.T, preferred_element_type=jnp.float32)
               + jnp.dot(d_up, w_up.T, preferred_element_type=jnp.float32)).astype(jnp.bfloat16)
    g_gate = jnp.dot(x_rows.T, d_gate, preferred_element_type=jnp.float32)
    g_up = jnp.dot(x_rows.T, d_up, preferred_element_type=jnp.float32)
    g_down = jnp.dot(hidden.T, dy_rows, preferred_element_type=jnp.float32)
    return y_rows, dx_rows, g_gate, g_up, g_down


def rounded_sum(terms):
    kept = lax.optimization_barrier(terms.astype(jnp.bfloat16))
    return jnp.sum(kept.astype(jnp.float32), axis=0).astype(jnp.bfloat16)


def reference(tokens, routes, gates, cotangent, w_gate, w_up, w_down):
    groups = N_DP
    sources = N_TENSOR * N_CONTEXT
    blocks = groups * sources
    width = tokens.shape[1]
    tok_blocks = tokens.reshape(blocks, TOK_DEV, width)
    cot_blocks = cotangent.reshape(blocks, TOK_DEV, width)
    route_blocks = routes.reshape(blocks, TOK_DEV, TOP)
    gate_blocks = gates.reshape(blocks, TOK_DEV, TOP)
    dest, owner, filled, weight = jax.vmap(lambda r, g: slot_tables(r, g, EXPERTS, CAP))(route_blocks, gate_blocks)
    picked = jax.vmap(lambda t, o: jnp.take(t, o, axis=0))(tok_blocks, owner)
    x_send = jnp.where((filled > 0)[:, :, None], picked, jnp.zeros_like(picked)).astype(jnp.bfloat16)
    pulled = jax.vmap(lambda t, o: jnp.take(t, o, axis=0))(cot_blocks, owner)
    dy_send = (weight[:, :, None] * pulled.astype(jnp.float32)).astype(jnp.bfloat16)

    def by_expert(buffer):
        shaped = buffer.reshape(groups, sources, EXPERTS, CAP, width)
        return shaped.transpose(2, 0, 1, 3, 4).reshape(EXPERTS, groups, sources * CAP, width)

    def one_expert(items):
        x_e, dy_e, wg, wu, wd = items
        y_e, dx_e, g_gate, g_up, g_down = jax.vmap(lambda a, b: expert_pass(a, b, wg, wu, wd))(x_e, dy_e)
        return y_e, dx_e, rounded_sum(g_gate), rounded_sum(g_up), rounded_sum(g_down)

    y_all, dx_all, grad_gate, grad_up, grad_down = lax.map(
        one_expert, (by_expert(x_send), by_expert(dy_send), w_gate, w_up, w_down))

    def by_block(rows):
        shaped = rows.reshape(EXPERTS, groups, sources, CAP, width)
        return shaped.transpose(1, 2, 0, 3, 4).reshape(blocks, EXPERTS * CAP, width)

    def combine(back, dst, scale):
        rows = jnp.take(back, dst, axis=0).reshape(TOK_DEV, TOP, width).astype(jnp.float32)
        return jnp.sum(scale[:, :, None] * rows, axis=1).astype(jnp.bfloat16)

    mixed = jax.vmap(combine)(by_block(y_all), dest, gate_blocks).reshape(tokens.shape)
    ones = jnp.ones_like(gate_blocks)
    d_tokens = jax.vmap(combine)(by_block(dx_all), dest, ones).reshape(tokens.shape)
    return mixed, d_tokens, grad_gate, grad_up, grad_down
```

```python
import functools

import jax
import jax.numpy as jnp
from jax import lax
from jax.experimental import pallas as pl
from jax.experimental.pallas import tpu as pltpu
from jax.sharding import PartitionSpec as P

MESH = pl.DeviceIdType.MESH
GROUPS = 4
EXPERTS = 32
CAP = 10
TOK = 128
SLAB = GROUPS * CAP
CHUNKS = 4
PER = EXPERTS // CHUNKS
ROWS = PER * SLAB
OWN = ROWS // GROUPS
SELF = 8

NT = (((1,), (1,)), ((), ()))
TN = (((0,), (0,)), ((), ()))


def dot(a, b):
    return jnp.dot(a, b, preferred_element_type=jnp.float32)


def kernel(
    tab_ref, tokens, cotangent, w_gate, w_up, w_down,
    mixed, d_tokens, g_gate, g_up, g_down,
    tb, tx, tc, oh, og, wg, wu, wd, sx, sy, rx, ry, by, bx, xs, ys, part, got, act, gu, gg,
    tab_s, tab_r, tx_s, tx_r, tc_s, tc_r, loc,
    sx_s, sx_r, sy_s, sy_r, bks_y, bkr_y, bks_x, bkr_x,
    rs1_s, rs1_r, rs2_s, rs2_r, ag1_s, ag1_r, ag2_s, ag2_r,
    fm_s, fm_r, fd_s, fd_r,
):
    d = lax.axis_index("dp")
    t = lax.axis_index("tensor")
    c = lax.axis_index("context")
    core = lax.rem(t, 2)
    py = (t // 2) * 2 + c // 4
    pz = lax.rem(c, 4)
    width = tx.shape[2]
    half = width // 2

    def offset(j):
        kpos, i = j // PER, lax.rem(j, PER)
        kk = lax.rem(2 + 2 * kpos + (kpos // 2) * 3, 4)
        z = lax.rem(i, 4)
        return i // 4, lax.rem(kk + 4 - z, 4), z

    def peer(j, sign):
        a, y, z = offset(j)
        if sign < 0:
            y, z = 4 - y, 4 - z
        y, z = lax.rem(py + y, 4), lax.rem(pz + z, 4)
        return (d, (y // 2) * 2 + lax.rem(core + a, 2), lax.rem(y, 2) * 4 + z)

    def ring(p):
        return (lax.rem(d + p, GROUPS), t, c)

    def remote(src, dst, s, r, dev):
        return pltpu.make_async_remote_copy(
            src_ref=src, dst_ref=dst, send_sem=s, recv_sem=r, device_id=dev, device_id_type=MESH
        )

    barrier = pltpu.get_barrier_semaphore()

    def greet(j, carry):
        @pl.when(j != SELF)
        def _():
            pl.semaphore_signal(barrier, inc=1, device_id=peer(j, 1), device_id_type=MESH)

        return carry

    lax.fori_loop(0, EXPERTS, greet, 0)
    for p in range(1, GROUPS):
        pl.semaphore_signal(barrier, inc=1, device_id=ring(p), device_id_type=MESH)
    pl.semaphore_wait(barrier, EXPERTS - 1 + GROUPS - 1)

    def columns(p):
        q = lax.rem(d + p, GROUPS)
        return pl.ds(pl.multiple_of(q * width, width), width)

    def dense(src, dst, s, r, p):
        return remote(src.at[:, columns(p)], dst.at[d], s.at[p - 1], r.at[p - 1], ring(p))

    own_tx = pltpu.make_async_copy(tokens.at[:, columns(0)], tx.at[d], loc.at[0])
    own_tc = pltpu.make_async_copy(cotangent.at[:, columns(0)], tc.at[d], loc.at[1])
    for p in range(1, GROUPS):
        dense(tokens, tx, tx_s, tx_r, p).start()
    own_tx.start()
    for p in range(1, GROUPS):
        dense(cotangent, tc, tc_s, tc_r, p).start()
    own_tc.start()
    weights = [
        pltpu.make_async_copy(w_gate.at[0], wg, loc.at[2]),
        pltpu.make_async_copy(w_up.at[0], wu, loc.at[3]),
        pltpu.make_async_copy(w_down.at[0], wd, loc.at[4]),
    ]
    for w in weights:
        w.start()

    e = lax.broadcasted_iota(jnp.int32, (EXPERTS, TOK), 0)
    e_core = (e >> 3) & 1
    e_y = (e >> 4) * 2 + ((e >> 2) & 1)
    e_z = e & 3
    oa = (e_core - core + 2) & 1
    oy = (e_y - py + 4) & 3
    oz = (e_z - pz + 4) & 3
    kk = (oy + oz) & 3
    kpos = jnp.where(kk == 2, 0, jnp.where(kk == 0, 1, jnp.where(kk == 1, 2, 3)))
    first_row = ((kpos * PER + oa * 4 + oz) * SLAB + d * CAP).astype(jnp.float32)
    e_f = e.astype(jnp.float32)
    tab = tab_ref[...]
    chosen0 = jnp.where(e_f == tab[0:1, :], 1.0, 0.0)
    chosen1 = jnp.where(e_f == tab[1:2, :], 1.0, 0.0)
    earlier = jnp.where(
        lax.broadcasted_iota(jnp.int32, (TOK, TOK), 0) < lax.broadcasted_iota(jnp.int32, (TOK, TOK), 1), 1.0, 0.0
    ).astype(jnp.bfloat16)
    before = dot((chosen0 + chosen1).astype(jnp.bfloat16), earlier)
    place = first_row + before
    key0 = jnp.sum(chosen0 * place, axis=0, keepdims=True)
    key1 = jnp.sum(chosen1 * place, axis=0, keepdims=True)
    tb[d] = jnp.concatenate([key0, key1, tab[2:4, :], jnp.zeros((4, TOK), jnp.float32)], axis=0)

    def tables(p):
        return remote(tb.at[d], tb.at[d], tab_s.at[p - 1], tab_r.at[p - 1], ring(p))

    for p in range(1, GROUPS):
        tables(p).start()
    for p in range(1, GROUPS):
        tables(p).wait()

    def halves(value):
        return [value[:, h * half : (h + 1) * half].reshape(PER, SLAB, half) for h in range(2)]

    def to_slabs(buf, k, value):
        for h, v in enumerate(halves(value)):
            buf[pl.ds(k * PER, PER), h * SLAB : (h + 1) * SLAB, :] = v.astype(jnp.bfloat16)

    def from_slabs(buf, k, h):
        v = buf[pl.ds(k * PER, PER), h * SLAB : (h + 1) * SLAB, :].astype(jnp.float32)
        return v.reshape(ROWS, half).astype(jnp.bfloat16)

    def slab_copy(src, dst, s, r, j, sign):
        return remote(src.at[j], dst.at[j], s.at[j], r.at[j], peer(j, sign))

    def each_slot(k, act_on):
        def body(i, carry):
            j = k * PER + i

            @pl.when(j != SELF)
            def _():
                act_on(j)

            return carry

        lax.fori_loop(0, PER, body, 0)

    def send_slabs(src, dst, s, r, k, sign):
        each_slot(k, lambda j: slab_copy(src, dst, s, r, j, sign).start())

        @pl.when(k == SELF // PER)
        def _():
            dst[SELF] = src[SELF]

    def await_slabs(src, dst, s, r, k, sign):
        each_slot(k, lambda j: slab_copy(src, dst, s, r, j, sign).wait_recv())

    def await_sent(src, dst, s, r, k, sign):
        each_slot(k, lambda j: slab_copy(src, dst, s, r, j, sign).wait_send())

    for p in range(1, GROUPS):
        dense(tokens, tx, tx_s, tx_r, p).wait()
    own_tx.wait()

    def send_x(k, carry):
        row = (lax.broadcasted_iota(jnp.int32, (ROWS, TOK), 0) + k * ROWS).astype(jnp.float32)
        for g in range(GROUPS):
            info = tb[g]
            hit0, hit1 = row == info[0:1, :], row == info[1:2, :]
            cols = slice(g * TOK, (g + 1) * TOK)
            oh[k, :, cols] = jnp.where(hit0 | hit1, 1.0, 0.0).astype(jnp.bfloat16)
            og[k, :, cols] = jnp.where(hit0, info[2:3, :], jnp.where(hit1, info[3:4, :], 0.0))
        to_slabs(sx, k, dot(oh[k], tx[...].reshape(GROUPS * TOK, width)))
        send_slabs(sx, rx, sx_s, sx_r, k, 1)
        return carry

    lax.fori_loop(0, CHUNKS, send_x, 0)

    for p in range(1, GROUPS):
        dense(cotangent, tc, tc_s, tc_r, p).wait()
    own_tc.wait()

    def send_dy(k, carry):
        weight = jnp.sum(og[k], axis=1, keepdims=True)
        to_slabs(sy, k, dot(oh[k], tc[...].reshape(GROUPS * TOK, width)) * weight)
        send_slabs(sy, ry, sy_s, sy_r, k, 1)
        return carry

    lax.fori_loop(0, CHUNKS, send_dy, 0)
    for w in weights:
        w.wait()

    def rs1(k, p):
        q = lax.rem(d + p, GROUPS)
        return remote(
            part.at[k, q, pl.ds(0, 2)], got.at[k, p - 1, pl.ds(0, 2)], rs1_s.at[k, p - 1], rs1_r.at[k, p - 1], ring(p)
        )

    def rs2(k, p):
        q = lax.rem(d + p, GROUPS)
        return remote(part.at[k, q, 2], got.at[k, p - 1, 2], rs2_s.at[k, p - 1], rs2_r.at[k, p - 1], ring(p))

    def ag1(k, p):
        return remote(act.at[0, k, d], act.at[0, k, d], ag1_s.at[k, p - 1], ag1_r.at[k, p - 1], ring(p))

    def ag2(k, p):
        own = act.at[pl.ds(1, 2), k, d]
        return remote(own, own, ag2_s.at[k, p - 1], ag2_r.at[k, p - 1], ring(p))

    def partial_sums(k, q, value):
        part[k, :, q] = value.astype(jnp.bfloat16).reshape(GROUPS, OWN, value.shape[1])

    def first(k, carry):
        await_slabs(sx, rx, sx_s, sx_r, k, 1)
        for h in range(2):
            xs[k, :, h * half : (h + 1) * half] = from_slabs(rx, k, h)
        partial_sums(k, 0, dot(xs[k], wg[...]))
        partial_sums(k, 1, dot(xs[k], wu[...]))
        for p in range(1, GROUPS):
            rs1(k, p).start()
        return carry

    lax.fori_loop(0, CHUNKS, first, 0)

    def reduced(k, q):
        total = part[k, d, q].astype(jnp.float32)
        for p in range(1, GROUPS):
            total += got[k, p - 1, q].astype(jnp.float32)
        return total

    def second(k, carry):
        for p in range(1, GROUPS):
            rs1(k, p).wait()
        gate_h, up_h = reduced(k, 0), reduced(k, 1)
        gu[k, 0] = gate_h
        gu[k, 1] = up_h
        act[0, k, d] = (gate_h * jax.nn.sigmoid(gate_h) * up_h).astype(jnp.bfloat16)
        for p in range(1, GROUPS):
            ag1(k, p).start()
        await_slabs(sy, ry, sy_s, sy_r, k, 1)
        for h in range(2):
            ys[k, :, h * half : (h + 1) * half] = from_slabs(ry, k, h)
        partial_sums(k, 2, lax.dot_general(ys[k], wd[...], NT, preferred_element_type=jnp.float32))
        for p in range(1, GROUPS):
            rs2(k, p).start()
        return carry

    lax.fori_loop(0, CHUNKS, second, 0)

    def whole(q, k):
        return act[q, k].reshape(ROWS, act.shape[4])

    def third(k, carry):
        for p in range(1, GROUPS):
            rs2(k, p).wait()
        d_h = reduced(k, 2)
        gate_h, up_h = gu[k, 0], gu[k, 1]
        sigma = jax.nn.sigmoid(gate_h)
        act[1, k, d] = (d_h * up_h * sigma * (1.0 + gate_h * (1.0 - sigma))).astype(jnp.bfloat16)
        act[2, k, d] = (d_h * (gate_h * sigma)).astype(jnp.bfloat16)
        for p in range(1, GROUPS):
            ag2(k, p).start()
        for p in range(1, GROUPS):
            ag1(k, p).wait()
        y = dot(whole(0, k), wd[...])
        await_sent(sx, rx, sx_s, sx_r, k, 1)
        to_slabs(sx, k, y)
        send_slabs(sx, by, bks_y, bkr_y, k, -1)
        return carry

    lax.fori_loop(0, CHUNKS, third, 0)

    def fourth(k, carry):
        for p in range(1, GROUPS):
            ag2(k, p).wait()
        dx = lax.dot_general(whole(1, k), wg[...], NT, preferred_element_type=jnp.float32)
        dx += lax.dot_general(whole(2, k), wu[...], NT, preferred_element_type=jnp.float32)
        await_sent(sy, ry, sy_s, sy_r, k, 1)
        to_slabs(sy, k, dx)
        send_slabs(sy, bx, bks_x, bkr_x, k, -1)
        return carry

    lax.fori_loop(0, CHUNKS, fourth, 0)

    block = 256

    def all_rows(q):
        return act[q].reshape(CHUNKS * ROWS, act.shape[4])

    def weight_grads(b, carry):
        cols = pl.ds(pl.multiple_of(b * block, block), block)
        x = xs[:, :, cols].reshape(CHUNKS * ROWS, block)
        gg[0, cols, :] = lax.dot_general(x, all_rows(1), TN, preferred_element_type=jnp.float32).astype(jnp.bfloat16)
        gg[1, cols, :] = lax.dot_general(x, all_rows(2), TN, preferred_element_type=jnp.float32).astype(jnp.bfloat16)
        return carry

    lax.fori_loop(0, width // block, weight_grads, 0)
    outs = [
        pltpu.make_async_copy(gg.at[0], g_gate.at[0], loc.at[2]),
        pltpu.make_async_copy(gg.at[1], g_up.at[0], loc.at[3]),
        pltpu.make_async_copy(wd, g_down.at[0], loc.at[4]),
    ]
    outs[0].start()
    outs[1].start()

    def down_grads(b, carry):
        cols = pl.ds(pl.multiple_of(b * block, block), block)
        dy = ys[:, :, cols].reshape(CHUNKS * ROWS, block)
        wd[:, cols] = lax.dot_general(all_rows(0), dy, TN, preferred_element_type=jnp.float32).astype(jnp.bfloat16)
        return carry

    lax.fori_loop(0, width // block, down_grads, 0)
    outs[2].start()

    def final(src, dst, s, r, p):
        q = lax.rem(d + p, GROUPS)
        own = dst.at[:, pl.ds(pl.multiple_of(d * width, width), width)]
        return remote(src.at[q], own, s.at[p - 1], r.at[p - 1], ring(p))

    def combine(buf, matrix, stage):
        for h in range(2):
            total = jnp.zeros((GROUPS * TOK, half), jnp.float32)
            for k in range(CHUNKS):
                total += lax.dot_general(matrix(k), from_slabs(buf, k, h), TN, preferred_element_type=jnp.float32)
            stage[:, :, h * half : (h + 1) * half] = total.astype(jnp.bfloat16).reshape(GROUPS, TOK, half)

    def own_out(src, dst, sem):
        return pltpu.make_async_copy(src.at[d], dst.at[:, columns(0)], sem)

    def back_y(k, carry):
        await_slabs(sx, by, bks_y, bkr_y, k, -1)
        await_sent(sx, by, bks_y, bkr_y, k, -1)
        return carry

    lax.fori_loop(0, CHUNKS, back_y, 0)
    combine(by, lambda k: og[k].astype(jnp.bfloat16), tx)
    for p in range(1, GROUPS):
        final(tx, mixed, fm_s, fm_r, p).start()
    own_out(tx, mixed, loc.at[0]).start()

    def back_x(k, carry):
        await_slabs(sy, bx, bks_x, bkr_x, k, -1)
        await_sent(sy, bx, bks_x, bkr_x, k, -1)
        return carry

    lax.fori_loop(0, CHUNKS, back_x, 0)
    combine(bx, lambda k: oh[k], tc)
    for p in range(1, GROUPS):
        final(tc, d_tokens, fd_s, fd_r, p).start()
    own_out(tc, d_tokens, loc.at[1]).start()
    for p in range(1, GROUPS):
        final(tx, mixed, fm_s, fm_r, p).wait()
        final(tc, d_tokens, fd_s, fd_r, p).wait()
    own_out(tx, mixed, loc.at[0]).wait()
    own_out(tc, d_tokens, loc.at[1]).wait()
    for o in outs:
        o.wait()


def shards(tokens, routes, gates, cotangent, w_gate, w_up, w_down):
    tok, full = tokens.shape
    ff = w_gate.shape[2]
    width = full // GROUPS
    bf16, f32 = jnp.bfloat16, jnp.float32
    tab = jnp.concatenate([routes.astype(f32), gates], axis=1).T
    hbm = pl.BlockSpec(memory_space=pl.ANY)
    vmem = pl.BlockSpec(memory_space=pltpu.VMEM)
    slabs = pltpu.VMEM((EXPERTS, 2 * SLAB, width // 2), bf16)
    sem = pltpu.SemaphoreType.DMA
    return pl.pallas_call(
        kernel,
        out_shape=(
            jax.ShapeDtypeStruct(tokens.shape, bf16),
            jax.ShapeDtypeStruct(tokens.shape, bf16),
            jax.ShapeDtypeStruct(w_gate.shape, bf16),
            jax.ShapeDtypeStruct(w_up.shape, bf16),
            jax.ShapeDtypeStruct(w_down.shape, bf16),
        ),
        in_specs=[vmem] + [hbm] * 5,
        out_specs=(hbm,) * 5,
        scratch_shapes=[
            pltpu.VMEM((GROUPS, 8, tok), f32),
            pltpu.VMEM((GROUPS, tok, width), bf16),
            pltpu.VMEM((GROUPS, tok, width), bf16),
            pltpu.VMEM((CHUNKS, ROWS, GROUPS * tok), bf16),
            pltpu.VMEM((CHUNKS, ROWS, GROUPS * tok), f32),
            pltpu.VMEM((width, ff), bf16),
            pltpu.VMEM((width, ff), bf16),
            pltpu.VMEM((ff, width), bf16),
            slabs, slabs, slabs, slabs, slabs, slabs,
            pltpu.VMEM((CHUNKS, ROWS, width), bf16),
            pltpu.VMEM((CHUNKS, ROWS, width), bf16),
            pltpu.VMEM((CHUNKS, GROUPS, 3, OWN, ff), bf16),
            pltpu.VMEM((CHUNKS, GROUPS - 1, 3, OWN, ff), bf16),
            pltpu.VMEM((3, CHUNKS, GROUPS, OWN, ff), bf16),
            pltpu.VMEM((CHUNKS, 2, OWN, ff), f32),
            pltpu.VMEM((2, width, ff), bf16),
            sem((3,)), sem((3,)), sem((3,)), sem((3,)), sem((3,)), sem((3,)), sem((5,)),
        ]
        + [sem((EXPERTS,))] * 8
        + [sem((CHUNKS, 3))] * 8
        + [sem((3,))] * 4,
        compiler_params=pltpu.CompilerParams(
            collective_id=0, has_side_effects=True, vmem_limit_bytes=62 * 2**20
        ),
        cost_estimate=pl.CostEstimate(flops=24 * 10**9, bytes_accessed=14 * 10**6, transcendentals=500000),
    )(tab, tokens, cotangent, w_gate, w_up, w_down)


def solution(mesh):
    placed = (
        P(("dp", "tensor", "context"), None),
        P(("dp", "tensor", "context"), None),
        P(("dp", "tensor", "context"), None),
        P(("dp", "tensor", "context"), None),
        P(("tensor", "context"), "dp", None),
        P(("tensor", "context"), "dp", None),
        P(("tensor", "context"), None, "dp"),
    )
    return jax.shard_map(
        shards,
        mesh=mesh,
        in_specs=placed,
        out_specs=(
            P(("dp", "tensor", "context"), None),
            P(("dp", "tensor", "context"), None),
            P(("tensor", "context"), "dp", None),
            P(("tensor", "context"), "dp", None),
            P(("tensor", "context"), None, "dp"),
        ),
        check_vma=False,
    )
```

```python
import functools

import jax
import jax.numpy as jnp
from jax import lax
from jax.experimental import pallas as pl
from jax.experimental.pallas import tpu as pltpu
from jax.sharding import PartitionSpec as P

MESH = pl.DeviceIdType.MESH
BACKY_FIRST = True
DY_AT = 1
Y_EARLY = True
GROUPS = 4
EXPERTS = 32
CAP = 10
TOK = 128
SLAB = GROUPS * CAP
CHUNKS = 4
PER = EXPERTS // CHUNKS
ROWS = PER * SLAB
OWN = ROWS // GROUPS
SELF = 8

NT = (((1,), (1,)), ((), ()))
TN = (((0,), (0,)), ((), ()))


def dot(a, b):
    return jnp.dot(a, b, preferred_element_type=jnp.float32)


def kernel(
    tab_ref, tokens, cotangent, w_gate, w_up, w_down,
    mixed, d_tokens, g_gate, g_up, g_down,
    tb, tx, tc, oh, og, wg, wu, wd, sx, sy, rx, ry, by, bx, xs, ys, part, got, relay, act, gu, gg,
    tab_s, tab_r, tx_s, tx_r, tc_s, tc_r, loc,
    sx_s, sx_r, sy_s, sy_r, bks_y, bkr_y, bks_x, bkr_x,
    rs_s, rs_r, ag_s, ag_r,
    fm_s, fm_r, fd_s, fd_r,
):
    d = lax.axis_index("dp")
    t = lax.axis_index("tensor")
    c = lax.axis_index("context")
    core = lax.rem(t, 2)
    py = (t // 2) * 2 + c // 4
    pz = lax.rem(c, 4)
    width = tx.shape[2]
    half = width // 2

    def offset(j):
        kpos, i = j // PER, lax.rem(j, PER)
        kk = lax.rem(2 + 2 * kpos + (kpos // 2) * 3, 4)
        z = lax.rem(i, 4)
        return i // 4, lax.rem(kk + 4 - z, 4), z

    def peer(j, sign):
        a, y, z = offset(j)
        if sign < 0:
            y, z = 4 - y, 4 - z
        y, z = lax.rem(py + y, 4), lax.rem(pz + z, 4)
        return (d, (y // 2) * 2 + lax.rem(core + a, 2), lax.rem(y, 2) * 4 + z)

    def ring(p):
        return (lax.rem(d + p, GROUPS), t, c)

    def remote(src, dst, s, r, dev):
        return pltpu.make_async_remote_copy(
            src_ref=src, dst_ref=dst, send_sem=s, recv_sem=r, device_id=dev, device_id_type=MESH
        )

    barrier = pltpu.get_barrier_semaphore()

    def greet(j, carry):
        @pl.when(j != SELF)
        def _():
            pl.semaphore_signal(barrier, inc=1, device_id=peer(j, 1), device_id_type=MESH)

        return carry

    lax.fori_loop(0, EXPERTS, greet, 0)
    for p in range(1, GROUPS):
        pl.semaphore_signal(barrier, inc=1, device_id=ring(p), device_id_type=MESH)

    e = lax.broadcasted_iota(jnp.int32, (EXPERTS, TOK), 0)
    e_core = (e >> 3) & 1
    e_y = (e >> 4) * 2 + ((e >> 2) & 1)
    e_z = e & 3
    oa = (e_core - core + 2) & 1
    oy = (e_y - py + 4) & 3
    oz = (e_z - pz + 4) & 3
    kk = (oy + oz) & 3
    kpos = jnp.where(kk == 2, 0, jnp.where(kk == 0, 1, jnp.where(kk == 1, 2, 3)))
    first_row = ((kpos * PER + oa * 4 + oz) * SLAB + d * CAP).astype(jnp.float32)
    e_f = e.astype(jnp.float32)
    tab = tab_ref[...]
    chosen0 = jnp.where(e_f == tab[0:1, :], 1.0, 0.0)
    chosen1 = jnp.where(e_f == tab[1:2, :], 1.0, 0.0)
    earlier = jnp.where(
        lax.broadcasted_iota(jnp.int32, (TOK, TOK), 0) < lax.broadcasted_iota(jnp.int32, (TOK, TOK), 1), 1.0, 0.0
    ).astype(jnp.bfloat16)
    before = dot((chosen0 + chosen1).astype(jnp.bfloat16), earlier)
    place = first_row + before
    key0 = jnp.sum(chosen0 * place, axis=0, keepdims=True)
    key1 = jnp.sum(chosen1 * place, axis=0, keepdims=True)
    tb[d] = jnp.concatenate([key0, key1, tab[2:4, :], jnp.zeros((4, TOK), jnp.float32)], axis=0)

    pl.semaphore_wait(barrier, EXPERTS - 1 + GROUPS - 1)

    def tables(p):
        return remote(tb.at[d], tb.at[d], tab_s.at[p - 1], tab_r.at[p - 1], ring(p))

    for p in range(1, GROUPS):
        tables(p).start()

    def columns(p):
        q = lax.rem(d + p, GROUPS)
        return pl.ds(pl.multiple_of(q * width, width), width)

    def dense(src, dst, s, r, p):
        return remote(src.at[:, columns(p)], dst.at[d], s.at[p - 1], r.at[p - 1], ring(p))

    own_tx = pltpu.make_async_copy(tokens.at[:, columns(0)], tx.at[d], loc.at[0])
    own_tc = pltpu.make_async_copy(cotangent.at[:, columns(0)], tc.at[d], loc.at[1])
    for p in range(1, GROUPS):
        dense(tokens, tx, tx_s, tx_r, p).start()
    own_tx.start()
    for p in range(1, GROUPS):
        dense(cotangent, tc, tc_s, tc_r, p).start()
    own_tc.start()
    weights = [
        pltpu.make_async_copy(w_gate.at[0], wg, loc.at[2]),
        pltpu.make_async_copy(w_up.at[0], wu, loc.at[3]),
        pltpu.make_async_copy(w_down.at[0], wd, loc.at[4]),
    ]
    for w in weights:
        w.start()

    for p in range(1, GROUPS):
        tables(p).wait()

    def halves(value):
        return [value[:, h * half : (h + 1) * half].reshape(PER, SLAB, half) for h in range(2)]

    def to_slabs(buf, k, value):
        for h, v in enumerate(halves(value)):
            buf[pl.ds(k * PER, PER), h * SLAB : (h + 1) * SLAB, :] = v.astype(jnp.bfloat16)

    def from_slabs(buf, k, h):
        v = buf[pl.ds(k * PER, PER), h * SLAB : (h + 1) * SLAB, :].astype(jnp.float32)
        return v.reshape(ROWS, half).astype(jnp.bfloat16)

    def slab_copy(src, dst, s, r, j, sign):
        return remote(src.at[j], dst.at[j], s.at[j // PER], r.at[j // PER], peer(j, sign))

    def each_slot(k, act_on):
        def body(i, carry):
            j = k * PER + i

            @pl.when(j != SELF)
            def _():
                act_on(j)

            return carry

        lax.fori_loop(0, PER, body, 0)

    def send_slabs(src, dst, s, r, k, sign):
        each_slot(k, lambda j: slab_copy(src, dst, s, r, j, sign).start())

        @pl.when(k == SELF // PER)
        def _():
            dst[SELF] = src[SELF]

    def await_bytes(buf, sem, k):
        @pl.when(k == SELF // PER)
        def _():
            ref = buf.at[pl.ds(SELF + 1, PER - 1)]
            pltpu.make_async_copy(ref, ref, sem.at[k]).wait()

        @pl.when(k != SELF // PER)
        def _():
            ref = buf.at[pl.ds(k * PER, PER)]
            pltpu.make_async_copy(ref, ref, sem.at[k]).wait()

    def await_slabs(src, dst, s, r, k, sign):
        await_bytes(dst, r, k)

    def await_sent(src, dst, s, r, k, sign):
        await_bytes(src, s, k)

    for p in range(1, GROUPS):
        dense(tokens, tx, tx_s, tx_r, p).wait()
    own_tx.wait()

    def send_x(k, carry):
        row = (lax.broadcasted_iota(jnp.int32, (ROWS, TOK), 0) + k * ROWS).astype(jnp.float32)
        for g in range(GROUPS):
            info = tb[g]
            hit0, hit1 = row == info[0:1, :], row == info[1:2, :]
            cols = slice(g * TOK, (g + 1) * TOK)
            oh[k, :, cols] = jnp.where(hit0 | hit1, 1.0, 0.0).astype(jnp.bfloat16)
            og[k, :, cols] = jnp.where(hit0, info[2:3, :], jnp.where(hit1, info[3:4, :], 0.0))
        to_slabs(sx, k, dot(oh[k], tx[...].reshape(GROUPS * TOK, width)))
        send_slabs(sx, rx, sx_s, sx_r, k, 1)
        return carry

    lax.fori_loop(0, CHUNKS, send_x, 0)

    def send_dy(k, carry):
        weight = jnp.sum(og[k], axis=1, keepdims=True)
        to_slabs(sy, k, dot(oh[k], tc[...].reshape(GROUPS * TOK, width)) * weight)
        send_slabs(sy, ry, sy_s, sy_r, k, 1)
        return carry

    def await_cot():
        for p in range(1, GROUPS):
            dense(cotangent, tc, tc_s, tc_r, p).wait()
        own_tc.wait()

    if DY_AT < 0:
        await_cot()
        lax.fori_loop(0, CHUNKS, send_dy, 0)
    for w in weights:
        w.wait()

    def way(k, q, mixed_q):
        if q == mixed_q:
            return 1 + 2 * lax.rem(k, 2)
        return 1 if q == min({0, 1, 2} - {mixed_q}) else 3

    def towards(n):
        return lax.rem(d + n, GROUPS)

    def rs(k, q, kind):
        w = way(k, q, 2)
        s, r = rs_s.at[0], rs_r.at[k, q, min(kind, 1)]
        if kind == 0:
            return remote(part.at[k, towards(2), q], relay.at[k, q], s, r, ring(w))
        if kind == 1:
            return remote(part.at[k, towards(4 - w), q], got.at[k, q, 0], s, r, ring(4 - w))
        return remote(part.at[k, towards(w), q], got.at[k, q, 1], s, r, ring(w))

    def rs_start(k, q):
        rs(k, q, 0).start()
        rs(k, q, 1).start()

    def rs_add(k, q):
        rs(k, q, 0).wait_recv()
        o = towards(way(k, q, 2))
        part[k, o, q] = (part[k, o, q].astype(jnp.float32) + relay[k, q].astype(jnp.float32)).astype(jnp.bfloat16)
        rs(k, q, 2).start()

    def rs_total(k, q):
        pltpu.make_async_copy(got.at[k, q], got.at[k, q], rs_r.at[k, q, 1]).wait()
        total = part[k, d, q].astype(jnp.float32)
        return total + got[k, q, 0].astype(jnp.float32) + got[k, q, 1].astype(jnp.float32)

    def ag(k, q, kind):
        w = way(k, q, 0)
        s, r = ag_s.at[0], ag_r.at[k, q, min(kind, 1)]
        o = d if kind < 2 else towards(4 - w)
        return remote(act.at[q, k, o], act.at[q, k, o], s, r, ring(w if kind != 1 else 4 - w))

    def ag_start(k, q):
        ag(k, q, 0).start()
        ag(k, q, 1).start()

    def ag_forward(k, q):
        ag(k, q, 0).wait_recv()
        ag(k, q, 2).start()

    def ag_whole(k, q):
        two = act.at[q, k, pl.ds(0, 2)]
        pltpu.make_async_copy(two, two, ag_r.at[k, q, 1]).wait()
        return act[q, k].reshape(ROWS, act.shape[4])

    def partial_sums(k, q, value):
        part[k, :, q] = value.astype(jnp.bfloat16).reshape(GROUPS, OWN, value.shape[1])

    def in_turn(step, later):
        def body(k, carry):
            step(k)

            @pl.when(k > 0)
            def _():
                later(k - 1)

            return carry

        lax.fori_loop(0, CHUNKS, body, 0)
        later(CHUNKS - 1)

    def first(k):
        await_slabs(sx, rx, sx_s, sx_r, k, 1)
        for h in range(2):
            xs[k, :, h * half : (h + 1) * half] = from_slabs(rx, k, h)
        partial_sums(k, 0, dot(xs[k], wg[...]))
        rs_start(k, 0)
        partial_sums(k, 1, dot(xs[k], wu[...]))
        rs_start(k, 1)
        if DY_AT >= 0:
            @pl.when(k == DY_AT)
            def _():
                await_cot()

            @pl.when(k >= DY_AT)
            def _():
                send_dy(k - DY_AT, 0)

    def first_later(k):
        rs_add(k, 0)
        rs_add(k, 1)

    in_turn(first, first_later)
    if DY_AT > 0:
        lax.fori_loop(CHUNKS - DY_AT, CHUNKS, send_dy, 0)

    def send_y(k):
        y = dot(ag_whole(k, 0), wd[...])
        await_sent(sx, rx, sx_s, sx_r, k, 1)
        to_slabs(sx, k, y)
        send_slabs(sx, by, bks_y, bkr_y, k, -1)

    def second(k):
        gate_h, up_h = rs_total(k, 0), rs_total(k, 1)
        gu[k, 0] = gate_h
        gu[k, 1] = up_h
        act[0, k, d] = (gate_h * jax.nn.sigmoid(gate_h) * up_h).astype(jnp.bfloat16)
        ag_start(k, 0)
        await_slabs(sy, ry, sy_s, sy_r, k, 1)
        for h in range(2):
            ys[k, :, h * half : (h + 1) * half] = from_slabs(ry, k, h)
        partial_sums(k, 2, lax.dot_general(ys[k], wd[...], NT, preferred_element_type=jnp.float32))
        rs_start(k, 2)

    def second_later(k):
        ag_forward(k, 0)
        rs_add(k, 2)
        if Y_EARLY:
            @pl.when(k > 0)
            def _():
                send_y(k - 1)

    in_turn(second, second_later)
    if Y_EARLY:
        send_y(CHUNKS - 1)

    def third(k):
        d_h = rs_total(k, 2)
        gate_h, up_h = gu[k, 0], gu[k, 1]
        sigma = jax.nn.sigmoid(gate_h)
        act[1, k, d] = (d_h * up_h * sigma * (1.0 + gate_h * (1.0 - sigma))).astype(jnp.bfloat16)
        ag_start(k, 1)
        act[2, k, d] = (d_h * (gate_h * sigma)).astype(jnp.bfloat16)
        ag_start(k, 2)
        if not Y_EARLY:
            send_y(k)

    def third_later(k):
        ag_forward(k, 1)
        ag_forward(k, 2)

    in_turn(third, third_later)

    def fourth(k, carry):
        dx = lax.dot_general(ag_whole(k, 1), wg[...], NT, preferred_element_type=jnp.float32)
        dx += lax.dot_general(ag_whole(k, 2), wu[...], NT, preferred_element_type=jnp.float32)
        await_sent(sy, ry, sy_s, sy_r, k, 1)
        to_slabs(sy, k, dx)
        send_slabs(sy, bx, bks_x, bkr_x, k, -1)
        return carry

    lax.fori_loop(0, CHUNKS, fourth, 0)

    def final(src, dst, s, r, p):
        q = lax.rem(d + p, GROUPS)
        own = dst.at[:, pl.ds(pl.multiple_of(d * width, width), width)]
        return remote(src.at[q], own, s.at[p - 1], r.at[p - 1], ring(p))

    def combine(buf, matrix, stage):
        for h in range(2):
            total = jnp.zeros((GROUPS * TOK, half), jnp.float32)
            for k in range(CHUNKS):
                total += lax.dot_general(matrix(k), from_slabs(buf, k, h), TN, preferred_element_type=jnp.float32)
            stage[:, :, h * half : (h + 1) * half] = total.astype(jnp.bfloat16).reshape(GROUPS, TOK, half)

    def own_out(src, dst, sem):
        return pltpu.make_async_copy(src.at[d], dst.at[:, columns(0)], sem)

    def finish_y():
        def back_y(k, carry):
            await_slabs(sx, by, bks_y, bkr_y, k, -1)
            await_sent(sx, by, bks_y, bkr_y, k, -1)
            return carry

        lax.fori_loop(0, CHUNKS, back_y, 0)
        combine(by, lambda k: og[k].astype(jnp.bfloat16), tx)
        for p in range(1, GROUPS):
            final(tx, mixed, fm_s, fm_r, p).start()
        own_out(tx, mixed, loc.at[0]).start()

    if BACKY_FIRST:
        finish_y()

    block = 256

    def all_rows(q):
        return act[q].reshape(CHUNKS * ROWS, act.shape[4])

    def weight_grads(b, carry):
        cols = pl.ds(pl.multiple_of(b * block, block), block)
        x = xs[:, :, cols].reshape(CHUNKS * ROWS, block)
        gg[0, cols, :] = lax.dot_general(x, all_rows(1), TN, preferred_element_type=jnp.float32).astype(jnp.bfloat16)
        gg[1, cols, :] = lax.dot_general(x, all_rows(2), TN, preferred_element_type=jnp.float32).astype(jnp.bfloat16)
        return carry

    lax.fori_loop(0, width // block, weight_grads, 0)
    outs = [
        pltpu.make_async_copy(gg.at[0], g_gate.at[0], loc.at[2]),
        pltpu.make_async_copy(gg.at[1], g_up.at[0], loc.at[3]),
        pltpu.make_async_copy(wd, g_down.at[0], loc.at[4]),
    ]
    outs[0].start()
    outs[1].start()

    def down_grads(b, carry):
        cols = pl.ds(pl.multiple_of(b * block, block), block)
        dy = ys[:, :, cols].reshape(CHUNKS * ROWS, block)
        wd[:, cols] = lax.dot_general(all_rows(0), dy, TN, preferred_element_type=jnp.float32).astype(jnp.bfloat16)
        return carry

    lax.fori_loop(0, width // block, down_grads, 0)
    outs[2].start()

    if not BACKY_FIRST:
        finish_y()

    def back_x(k, carry):
        await_slabs(sy, bx, bks_x, bkr_x, k, -1)
        await_sent(sy, bx, bks_x, bkr_x, k, -1)
        return carry

    lax.fori_loop(0, CHUNKS, back_x, 0)
    combine(bx, lambda k: oh[k], tc)
    for p in range(1, GROUPS):
        final(tc, d_tokens, fd_s, fd_r, p).start()
    own_out(tc, d_tokens, loc.at[1]).start()
    for p in range(1, GROUPS):
        final(tx, mixed, fm_s, fm_r, p).wait()
        final(tc, d_tokens, fd_s, fd_r, p).wait()
    own_out(tx, mixed, loc.at[0]).wait()
    own_out(tc, d_tokens, loc.at[1]).wait()
    for o in outs:
        o.wait()
    sums, gathers = part.at[pl.ds(0, 3)], act.at[:, pl.ds(0, 3)]
    pltpu.make_async_copy(sums, sums, rs_s.at[0]).wait()
    pltpu.make_async_copy(gathers, gathers, ag_s.at[0]).wait()


def publish(*refs):
    for i in range(5):
        refs[5 + i][...] = refs[i][...]


def shards(tokens, routes, gates, cotangent, w_gate, w_up, w_down):
    tok, full = tokens.shape
    ff = w_gate.shape[2]
    width = full // GROUPS
    bf16, f32 = jnp.bfloat16, jnp.float32
    tab = jnp.concatenate([routes.astype(f32), gates], axis=1).T
    hbm = pl.BlockSpec(memory_space=pl.ANY)
    vmem = pl.BlockSpec(memory_space=pltpu.VMEM)
    slabs = pltpu.VMEM((EXPERTS, 2 * SLAB, width // 2), bf16)
    sem = pltpu.SemaphoreType.DMA
    results = pl.pallas_call(
        kernel,
        out_shape=(
            jax.ShapeDtypeStruct(tokens.shape, bf16),
            jax.ShapeDtypeStruct(tokens.shape, bf16),
            jax.ShapeDtypeStruct(w_gate.shape, bf16),
            jax.ShapeDtypeStruct(w_up.shape, bf16),
            jax.ShapeDtypeStruct(w_down.shape, bf16),
        ),
        in_specs=[vmem] + [hbm] * 5,
        out_specs=(hbm,) * 5,
        scratch_shapes=[
            pltpu.VMEM((GROUPS, 8, tok), f32),
            pltpu.VMEM((GROUPS, tok, width), bf16),
            pltpu.VMEM((GROUPS, tok, width), bf16),
            pltpu.VMEM((CHUNKS, ROWS, GROUPS * tok), bf16),
            pltpu.VMEM((CHUNKS, ROWS, GROUPS * tok), f32),
            pltpu.VMEM((width, ff), bf16),
            pltpu.VMEM((width, ff), bf16),
            pltpu.VMEM((ff, width), bf16),
            slabs, slabs, slabs, slabs, slabs, slabs,
            pltpu.VMEM((CHUNKS, ROWS, width), bf16),
            pltpu.VMEM((CHUNKS, ROWS, width), bf16),
            pltpu.VMEM((CHUNKS, GROUPS, 3, OWN, ff), bf16),
            pltpu.VMEM((CHUNKS, 3, 2, OWN, ff), bf16),
            pltpu.VMEM((CHUNKS, 3, OWN, ff), bf16),
            pltpu.VMEM((3, CHUNKS, GROUPS, OWN, ff), bf16),
            pltpu.VMEM((CHUNKS, 2, OWN, ff), f32),
            pltpu.VMEM((2, width, ff), bf16),
            sem((3,)), sem((3,)), sem((3,)), sem((3,)), sem((3,)), sem((3,)), sem((5,)),
        ]
        + [sem((CHUNKS,))] * 8
        + [sem((1,)), sem((CHUNKS, 3, 2)), sem((1,)), sem((CHUNKS, 3, 2))]
        + [sem((3,))] * 4,
        compiler_params=pltpu.CompilerParams(
            collective_id=0, has_side_effects=True, vmem_limit_bytes=62 * 2**20
        ),
        cost_estimate=pl.CostEstimate(flops=24 * 10**9, bytes_accessed=14 * 10**6, transcendentals=500000),
    )(tab, tokens, cotangent, w_gate, w_up, w_down)
    specs = [
        pl.BlockSpec((16, 4096), lambda i: (i, 0)),
        pl.BlockSpec((16, 4096), lambda i: (i, 0)),
        pl.BlockSpec((1, 128, 768), lambda i: (0, i, 0)),
        pl.BlockSpec((1, 128, 768), lambda i: (0, i, 0)),
        pl.BlockSpec((1, 96, 1024), lambda i: (0, i, 0)),
    ]
    return pl.pallas_call(
        publish,
        out_shape=[jax.ShapeDtypeStruct(r.shape, r.dtype) for r in results],
        grid=(8,),
        in_specs=specs,
        out_specs=specs,
    )(*results)


def solution(mesh):
    placed = (
        P(("dp", "tensor", "context"), None),
        P(("dp", "tensor", "context"), None),
        P(("dp", "tensor", "context"), None),
        P(("dp", "tensor", "context"), None),
        P(("tensor", "context"), "dp", None),
        P(("tensor", "context"), "dp", None),
        P(("tensor", "context"), None, "dp"),
    )
    return jax.shard_map(
        shards,
        mesh=mesh,
        in_specs=placed,
        out_specs=(
            P(("dp", "tensor", "context"), None),
            P(("dp", "tensor", "context"), None),
            P(("tensor", "context"), "dp", None),
            P(("tensor", "context"), "dp", None),
            P(("tensor", "context"), None, "dp"),
        ),
        check_vma=False,
    )
```

```python
import functools

import jax
import jax.numpy as jnp
from jax import lax
from jax.experimental import pallas as pl
from jax.experimental.pallas import tpu as pltpu
from jax.sharding import PartitionSpec as P

MESH = pl.DeviceIdType.MESH
DY_AT = 1
GROUPS = 4
EXPERTS = 32
CAP = 10
TOK = 128
SLAB = GROUPS * CAP
CHUNKS = 4
PER = EXPERTS // CHUNKS
ROWS = PER * SLAB
OWN = ROWS // GROUPS
SELF = 8

NT = (((1,), (1,)), ((), ()))
TN = (((0,), (0,)), ((), ()))


def dot(a, b):
    return jnp.dot(a, b, preferred_element_type=jnp.float32)


def kernel(
    tab_ref, tokens, cotangent, w_gate, w_up, w_down,
    mixed, d_tokens, g_gate, g_up, g_down,
    tb, tx, tc, oh, og, wg, wu, wd, sx, sy, rx, ry, by, bx, xs, ys, part, got, relay, act, gu, gg,
    tab_s, tab_r, tx_s, tx_r, tc_s, tc_r, loc,
    sx_s, sx_r, sy_s, sy_r, bks_y, bkr_y, bks_x, bkr_x,
    rs_s, rs_r, ag_s, ag_r,
    fm_s, fm_r, fd_s, fd_r,
):
    d = lax.axis_index("dp")
    t = lax.axis_index("tensor")
    c = lax.axis_index("context")
    core = lax.rem(t, 2)
    py = (t // 2) * 2 + c // 4
    pz = lax.rem(c, 4)
    width = tx.shape[2]
    half = width // 2

    def offset(j):
        kpos, i = j // PER, lax.rem(j, PER)
        kk = lax.rem(2 + 2 * kpos + (kpos // 2) * 3, 4)
        z = lax.rem(i, 4)
        return i // 4, lax.rem(kk + 4 - z, 4), z

    def peer(j, sign):
        a, y, z = offset(j)
        if sign < 0:
            y, z = 4 - y, 4 - z
        y, z = lax.rem(py + y, 4), lax.rem(pz + z, 4)
        return (d, (y // 2) * 2 + lax.rem(core + a, 2), lax.rem(y, 2) * 4 + z)

    def ring(p):
        return (lax.rem(d + p, GROUPS), t, c)

    def remote(src, dst, s, r, dev):
        return pltpu.make_async_remote_copy(
            src_ref=src, dst_ref=dst, send_sem=s, recv_sem=r, device_id=dev, device_id_type=MESH
        )

    barrier = pltpu.get_barrier_semaphore()

    def greet(j, carry):
        @pl.when(j != SELF)
        def _():
            pl.semaphore_signal(barrier, inc=1, device_id=peer(j, 1), device_id_type=MESH)

        return carry

    lax.fori_loop(0, EXPERTS, greet, 0)
    for p in range(1, GROUPS):
        pl.semaphore_signal(barrier, inc=1, device_id=ring(p), device_id_type=MESH)

    e = lax.broadcasted_iota(jnp.int32, (EXPERTS, TOK), 0)
    e_core = (e >> 3) & 1
    e_y = (e >> 4) * 2 + ((e >> 2) & 1)
    e_z = e & 3
    oa = (e_core - core + 2) & 1
    oy = (e_y - py + 4) & 3
    oz = (e_z - pz + 4) & 3
    kk = (oy + oz) & 3
    kpos = jnp.where(kk == 2, 0, jnp.where(kk == 0, 1, jnp.where(kk == 1, 2, 3)))
    first_row = ((kpos * PER + oa * 4 + oz) * SLAB + d * CAP).astype(jnp.float32)
    e_f = e.astype(jnp.float32)
    tab = tab_ref[...]
    chosen0 = jnp.where(e_f == tab[0:1, :], 1.0, 0.0)
    chosen1 = jnp.where(e_f == tab[1:2, :], 1.0, 0.0)
    earlier = jnp.where(
        lax.broadcasted_iota(jnp.int32, (TOK, TOK), 0) < lax.broadcasted_iota(jnp.int32, (TOK, TOK), 1), 1.0, 0.0
    ).astype(jnp.bfloat16)
    before = dot((chosen0 + chosen1).astype(jnp.bfloat16), earlier)
    place = first_row + before
    key0 = jnp.sum(chosen0 * place, axis=0, keepdims=True)
    key1 = jnp.sum(chosen1 * place, axis=0, keepdims=True)
    tb[d] = jnp.concatenate([key0, key1, tab[2:4, :], jnp.zeros((4, TOK), jnp.float32)], axis=0)

    pl.semaphore_wait(barrier, EXPERTS - 1 + GROUPS - 1)

    def tables(p):
        return remote(tb.at[d], tb.at[d], tab_s.at[p - 1], tab_r.at[p - 1], ring(p))

    for p in range(1, GROUPS):
        tables(p).start()

    def columns(p):
        q = lax.rem(d + p, GROUPS)
        return pl.ds(pl.multiple_of(q * width, width), width)

    def dense(src, dst, s, r, p):
        return remote(src.at[:, columns(p)], dst.at[d], s.at[p - 1], r.at[p - 1], ring(p))

    own_tx = pltpu.make_async_copy(tokens.at[:, columns(0)], tx.at[d], loc.at[0])
    own_tc = pltpu.make_async_copy(cotangent.at[:, columns(0)], tc.at[d], loc.at[1])
    for p in range(1, GROUPS):
        dense(tokens, tx, tx_s, tx_r, p).start()
    own_tx.start()
    for p in range(1, GROUPS):
        dense(cotangent, tc, tc_s, tc_r, p).start()
    own_tc.start()
    weights = [
        pltpu.make_async_copy(w_gate.at[0], wg, loc.at[2]),
        pltpu.make_async_copy(w_up.at[0], wu, loc.at[3]),
        pltpu.make_async_copy(w_down.at[0], wd, loc.at[4]),
    ]
    for w in weights:
        w.start()

    for p in range(1, GROUPS):
        tables(p).wait()

    def halves(value):
        return [value[:, h * half : (h + 1) * half].reshape(PER, SLAB, half) for h in range(2)]

    def to_slabs(buf, k, value):
        for h, v in enumerate(halves(value)):
            buf[pl.ds(k * PER, PER), h * SLAB : (h + 1) * SLAB, :] = v.astype(jnp.bfloat16)

    def from_slabs(buf, k, h):
        v = buf[pl.ds(k * PER, PER), h * SLAB : (h + 1) * SLAB, :].astype(jnp.float32)
        return v.reshape(ROWS, half).astype(jnp.bfloat16)

    def slab_copy(src, dst, s, r, j, sign):
        return remote(src.at[j], dst.at[j], s.at[j // PER], r.at[j // PER], peer(j, sign))

    def each_slot(k, act_on):
        def body(i, carry):
            j = k * PER + i

            @pl.when(j != SELF)
            def _():
                act_on(j)

            return carry

        lax.fori_loop(0, PER, body, 0)

    def send_slabs(src, dst, s, r, k, sign):
        each_slot(k, lambda j: slab_copy(src, dst, s, r, j, sign).start())

        @pl.when(k == SELF // PER)
        def _():
            dst[SELF] = src[SELF]

    def await_bytes(buf, sem, k):
        @pl.when(k == SELF // PER)
        def _():
            ref = buf.at[pl.ds(SELF + 1, PER - 1)]
            pltpu.make_async_copy(ref, ref, sem.at[k]).wait()

        @pl.when(k != SELF // PER)
        def _():
            ref = buf.at[pl.ds(k * PER, PER)]
            pltpu.make_async_copy(ref, ref, sem.at[k]).wait()

    def await_slabs(src, dst, s, r, k, sign):
        await_bytes(dst, r, k)

    def await_sent(src, dst, s, r, k, sign):
        await_bytes(src, s, k)

    for p in range(1, GROUPS):
        dense(tokens, tx, tx_s, tx_r, p).wait()
    own_tx.wait()

    def send_x(k, carry):
        row = (lax.broadcasted_iota(jnp.int32, (ROWS, TOK), 0) + k * ROWS).astype(jnp.float32)
        for g in range(GROUPS):
            info = tb[g]
            hit0, hit1 = row == info[0:1, :], row == info[1:2, :]
            cols = slice(g * TOK, (g + 1) * TOK)
            oh[k, :, cols] = jnp.where(hit0 | hit1, 1.0, 0.0).astype(jnp.bfloat16)
            og[k, :, cols] = jnp.where(hit0, info[2:3, :], jnp.where(hit1, info[3:4, :], 0.0))
        to_slabs(sx, k, dot(oh[k], tx[...].reshape(GROUPS * TOK, width)))
        send_slabs(sx, rx, sx_s, sx_r, k, 1)
        return carry

    lax.fori_loop(0, CHUNKS, send_x, 0)

    def send_dy(k):
        weight = jnp.sum(og[k], axis=1, keepdims=True)
        to_slabs(sy, k, dot(oh[k], tc[...].reshape(GROUPS * TOK, width)) * weight)
        send_slabs(sy, ry, sy_s, sy_r, k, 1)

    def await_cot():
        for p in range(1, GROUPS):
            dense(cotangent, tc, tc_s, tc_r, p).wait()
        own_tc.wait()

    for w in weights:
        w.wait()

    def way(k, q, mixed_q):
        if q == mixed_q:
            return 1 + 2 * lax.rem(k, 2)
        return 1 if q == min({0, 1, 2} - {mixed_q}) else 3

    def towards(n):
        return lax.rem(d + n, GROUPS)

    def rs(k, q, kind):
        w = way(k, q, 2)
        s, r = rs_s.at[0], rs_r.at[k, q, min(kind, 1)]
        if kind == 0:
            return remote(part.at[k, towards(2), q], relay.at[k, q], s, r, ring(w))
        if kind == 1:
            return remote(part.at[k, towards(4 - w), q], got.at[k, q, 0], s, r, ring(4 - w))
        return remote(part.at[k, towards(w), q], got.at[k, q, 1], s, r, ring(w))

    def rs_start(k, q):
        rs(k, q, 0).start()
        rs(k, q, 1).start()

    def rs_add(k, q):
        rs(k, q, 0).wait_recv()
        o = towards(way(k, q, 2))
        part[k, o, q] = (part[k, o, q].astype(jnp.float32) + relay[k, q].astype(jnp.float32)).astype(jnp.bfloat16)
        rs(k, q, 2).start()

    def rs_total(k, q):
        pltpu.make_async_copy(got.at[k, q], got.at[k, q], rs_r.at[k, q, 1]).wait()
        total = part[k, d, q].astype(jnp.float32)
        return total + got[k, q, 0].astype(jnp.float32) + got[k, q, 1].astype(jnp.float32)

    def ag(k, q, kind):
        w = way(k, q, 0)
        s, r = ag_s.at[0], ag_r.at[k, q, min(kind, 1)]
        o = d if kind < 2 else towards(4 - w)
        return remote(act.at[q, k, o], act.at[q, k, o], s, r, ring(w if kind != 1 else 4 - w))

    def ag_start(k, q):
        ag(k, q, 0).start()
        ag(k, q, 1).start()

    def ag_forward(k, q):
        ag(k, q, 0).wait_recv()
        ag(k, q, 2).start()

    def ag_whole(k, q):
        two = act.at[q, k, pl.ds(0, 2)]
        pltpu.make_async_copy(two, two, ag_r.at[k, q, 1]).wait()
        return act[q, k].reshape(ROWS, act.shape[4])

    def partial_sums(k, q, value):
        part[k, :, q] = value.astype(jnp.bfloat16).reshape(GROUPS, OWN, value.shape[1])

    def first(k):
        await_slabs(sx, rx, sx_s, sx_r, k, 1)
        for h in range(2):
            xs[k, :, h * half : (h + 1) * half] = from_slabs(rx, k, h)
        partial_sums(k, 0, dot(xs[k], wg[...]))
        rs_start(k, 0)
        partial_sums(k, 1, dot(xs[k], wu[...]))
        rs_start(k, 1)

    def first_add(k):
        rs_add(k, 0)
        rs_add(k, 1)

    def first_total(k):
        gate_h, up_h = rs_total(k, 0), rs_total(k, 1)
        gu[k, 0] = gate_h
        gu[k, 1] = up_h
        act[0, k, d] = (gate_h * jax.nn.sigmoid(gate_h) * up_h).astype(jnp.bfloat16)
        ag_start(k, 0)

    def second(k):
        await_slabs(sy, ry, sy_s, sy_r, k, 1)
        for h in range(2):
            ys[k, :, h * half : (h + 1) * half] = from_slabs(ry, k, h)
        partial_sums(k, 2, lax.dot_general(ys[k], wd[...], NT, preferred_element_type=jnp.float32))
        rs_start(k, 2)

    def second_total(k):
        d_h = rs_total(k, 2)
        gate_h, up_h = gu[k, 0], gu[k, 1]
        sigma = jax.nn.sigmoid(gate_h)
        act[1, k, d] = (d_h * up_h * sigma * (1.0 + gate_h * (1.0 - sigma))).astype(jnp.bfloat16)
        ag_start(k, 1)
        act[2, k, d] = (d_h * (gate_h * sigma)).astype(jnp.bfloat16)
        ag_start(k, 2)

    def second_forward(k):
        ag_forward(k, 1)
        ag_forward(k, 2)

    def send_y(k):
        y = dot(ag_whole(k, 0), wd[...])
        await_sent(sx, rx, sx_s, sx_r, k, 1)
        to_slabs(sx, k, y)
        send_slabs(sx, by, bks_y, bkr_y, k, -1)

    def send_dx(k):
        dx = lax.dot_general(ag_whole(k, 1), wg[...], NT, preferred_element_type=jnp.float32)
        dx += lax.dot_general(ag_whole(k, 2), wu[...], NT, preferred_element_type=jnp.float32)
        await_sent(sy, ry, sy_s, sy_r, k, 1)
        to_slabs(sy, k, dx)
        send_slabs(sy, bx, bks_x, bkr_x, k, -1)

    def final(src, dst, s, r, p, h):
        cols = pl.ds(pl.multiple_of(d * width + h * half, half), half)
        out = src.at[lax.rem(d + p, GROUPS), :, pl.ds(h * half, half)]
        return remote(out, dst.at[:, cols], s.at[p - 1, h], r.at[p - 1, h], ring(p))

    def combine(buf, arrived, matrix, stage, dst, s, r):
        for h in range(2):
            total = jnp.zeros((GROUPS * TOK, half), jnp.float32)
            for k in range(CHUNKS):
                if h == 0:
                    await_bytes(buf, arrived, jnp.int32(k))
                total += lax.dot_general(matrix(k), from_slabs(buf, k, h), TN, preferred_element_type=jnp.float32)
            stage[:, :, h * half : (h + 1) * half] = total.astype(jnp.bfloat16).reshape(GROUPS, TOK, half)
            for p in (2, 1, 3):
                final(stage, dst, s, r, p, h).start()

    def own_out(src, dst, sem):
        return pltpu.make_async_copy(src.at[d], dst.at[:, columns(0)], sem)

    def finish_y():
        combine(by, bkr_y, lambda k: og[k].astype(jnp.bfloat16), tx, mixed, fm_s, fm_r)
        own_out(tx, mixed, loc.at[0]).start()

    stages = (
        (0, first),
        (DY_AT, send_dy),
        (1, first_add),
        (2, first_total),
        (3, lambda k: ag_forward(k, 0)),
        (4, send_y),
        (5, lambda k: rs_add(k, 2)),
        (6, second_total),
        (7, second_forward),
        (8, send_dx),
        (4, second),
    )
    last = CHUNKS - 1 + max(lag for lag, _ in stages)

    def step(now, carry):
        @pl.when(now == DY_AT)
        def _():
            await_cot()

        @pl.when(now == last)
        def _():
            finish_y()

        for lag, stage in stages:
            pl.when((now >= lag) & (now < lag + CHUNKS))(functools.partial(stage, now - lag))
        return carry

    lax.fori_loop(0, last + 1, step, 0)

    block = 256

    def all_rows(q):
        return act[q].reshape(CHUNKS * ROWS, act.shape[4])

    def weight_grads(b, carry):
        cols = pl.ds(pl.multiple_of(b * block, block), block)
        x = xs[:, :, cols].reshape(CHUNKS * ROWS, block)
        gg[0, cols, :] = lax.dot_general(x, all_rows(1), TN, preferred_element_type=jnp.float32).astype(jnp.bfloat16)
        gg[1, cols, :] = lax.dot_general(x, all_rows(2), TN, preferred_element_type=jnp.float32).astype(jnp.bfloat16)
        return carry

    lax.fori_loop(0, width // block, weight_grads, 0)
    outs = [
        pltpu.make_async_copy(gg.at[0], g_gate.at[0], loc.at[2]),
        pltpu.make_async_copy(gg.at[1], g_up.at[0], loc.at[3]),
        pltpu.make_async_copy(wd, g_down.at[0], loc.at[4]),
    ]
    outs[0].start()
    outs[1].start()

    def down_grads(b, carry):
        cols = pl.ds(pl.multiple_of(b * block, block), block)
        dy = ys[:, :, cols].reshape(CHUNKS * ROWS, block)
        wd[:, cols] = lax.dot_general(all_rows(0), dy, TN, preferred_element_type=jnp.float32).astype(jnp.bfloat16)
        return carry

    lax.fori_loop(0, width // block, down_grads, 0)
    outs[2].start()

    combine(bx, bkr_x, lambda k: oh[k], tc, d_tokens, fd_s, fd_r)
    own_out(tc, d_tokens, loc.at[1]).start()
    for p in range(1, GROUPS):
        for h in range(2):
            final(tx, mixed, fm_s, fm_r, p, h).wait()
            final(tc, d_tokens, fd_s, fd_r, p, h).wait()
    own_out(tx, mixed, loc.at[0]).wait()
    own_out(tc, d_tokens, loc.at[1]).wait()
    for o in outs:
        o.wait()

    def back_sent(k, carry):
        await_bytes(sx, bks_y, k)
        await_bytes(sy, bks_x, k)
        return carry

    lax.fori_loop(0, CHUNKS, back_sent, 0)
    sums, gathers = part.at[pl.ds(0, 3)], act.at[:, pl.ds(0, 3)]
    pltpu.make_async_copy(sums, sums, rs_s.at[0]).wait()
    pltpu.make_async_copy(gathers, gathers, ag_s.at[0]).wait()


def publish(*refs):
    for i in range(5):
        refs[5 + i][...] = refs[i][...]


def shards(tokens, routes, gates, cotangent, w_gate, w_up, w_down):
    tok, full = tokens.shape
    ff = w_gate.shape[2]
    width = full // GROUPS
    bf16, f32 = jnp.bfloat16, jnp.float32
    tab = jnp.concatenate([routes.astype(f32), gates], axis=1).T
    hbm = pl.BlockSpec(memory_space=pl.ANY)
    vmem = pl.BlockSpec(memory_space=pltpu.VMEM)
    slabs = pltpu.VMEM((EXPERTS, 2 * SLAB, width // 2), bf16)
    sem = pltpu.SemaphoreType.DMA
    results = pl.pallas_call(
        kernel,
        out_shape=(
            jax.ShapeDtypeStruct(tokens.shape, bf16),
            jax.ShapeDtypeStruct(tokens.shape, bf16),
            jax.ShapeDtypeStruct(w_gate.shape, bf16),
            jax.ShapeDtypeStruct(w_up.shape, bf16),
            jax.ShapeDtypeStruct(w_down.shape, bf16),
        ),
        in_specs=[vmem] + [hbm] * 5,
        out_specs=(hbm,) * 5,
        scratch_shapes=[
            pltpu.VMEM((GROUPS, 8, tok), f32),
            pltpu.VMEM((GROUPS, tok, width), bf16),
            pltpu.VMEM((GROUPS, tok, width), bf16),
            pltpu.VMEM((CHUNKS, ROWS, GROUPS * tok), bf16),
            pltpu.VMEM((CHUNKS, ROWS, GROUPS * tok), f32),
            pltpu.VMEM((width, ff), bf16),
            pltpu.VMEM((width, ff), bf16),
            pltpu.VMEM((ff, width), bf16),
            slabs, slabs, slabs, slabs, slabs, slabs,
            pltpu.VMEM((CHUNKS, ROWS, width), bf16),
            pltpu.VMEM((CHUNKS, ROWS, width), bf16),
            pltpu.VMEM((CHUNKS, GROUPS, 3, OWN, ff), bf16),
            pltpu.VMEM((CHUNKS, 3, 2, OWN, ff), bf16),
            pltpu.VMEM((CHUNKS, 3, OWN, ff), bf16),
            pltpu.VMEM((3, CHUNKS, GROUPS, OWN, ff), bf16),
            pltpu.VMEM((CHUNKS, 2, OWN, ff), f32),
            pltpu.VMEM((2, width, ff), bf16),
            sem((3,)), sem((3,)), sem((3,)), sem((3,)), sem((3,)), sem((3,)), sem((5,)),
        ]
        + [sem((CHUNKS,))] * 8
        + [sem((1,)), sem((CHUNKS, 3, 2)), sem((1,)), sem((CHUNKS, 3, 2))]
        + [sem((3, 2))] * 4,
        compiler_params=pltpu.CompilerParams(
            collective_id=0, has_side_effects=True, vmem_limit_bytes=62 * 2**20
        ),
        cost_estimate=pl.CostEstimate(flops=24 * 10**9, bytes_accessed=14 * 10**6, transcendentals=500000),
    )(tab, tokens, cotangent, w_gate, w_up, w_down)
    specs = [
        pl.BlockSpec((32, 4096), lambda i: (i, 0)),
        pl.BlockSpec((32, 4096), lambda i: (i, 0)),
        pl.BlockSpec((1, 256, 768), lambda i: (0, i, 0)),
        pl.BlockSpec((1, 256, 768), lambda i: (0, i, 0)),
        pl.BlockSpec((1, 192, 1024), lambda i: (0, i, 0)),
    ]
    return pl.pallas_call(
        publish,
        out_shape=[jax.ShapeDtypeStruct(r.shape, r.dtype) for r in results],
        grid=(4,),
        in_specs=specs,
        out_specs=specs,
    )(*results)


def solution(mesh):
    placed = (
        P(("dp", "tensor", "context"), None),
        P(("dp", "tensor", "context"), None),
        P(("dp", "tensor", "context"), None),
        P(("dp", "tensor", "context"), None),
        P(("tensor", "context"), "dp", None),
        P(("tensor", "context"), "dp", None),
        P(("tensor", "context"), None, "dp"),
    )
    return jax.shard_map(
        shards,
        mesh=mesh,
        in_specs=placed,
        out_specs=(
            P(("dp", "tensor", "context"), None),
            P(("dp", "tensor", "context"), None),
            P(("tensor", "context"), "dp", None),
            P(("tensor", "context"), "dp", None),
            P(("tensor", "context"), None, "dp"),
        ),
        check_vma=False,
    )
```

```python
import functools

import jax
import jax.numpy as jnp
from jax import lax
from jax.experimental import pallas as pl
from jax.experimental.pallas import tpu as pltpu
from jax.sharding import PartitionSpec as P

MESH = pl.DeviceIdType.MESH
DY_AT = 1
GROUPS = 4
EXPERTS = 32
CAP = 10
TOK = 128
SLAB = GROUPS * CAP
CHUNKS = 4
PER = EXPERTS // CHUNKS
ROWS = PER * SLAB
OWN = ROWS // GROUPS
SELF = 8

NT = (((1,), (1,)), ((), ()))
TN = (((0,), (0,)), ((), ()))


def dot(a, b):
    return jnp.dot(a, b, preferred_element_type=jnp.float32)


def kernel(
    tab_ref, tokens, cotangent, w_gate, w_up, w_down,
    mixed, d_tokens, g_gate, g_up, g_down,
    tb, tx, tc, oh, og, wg, wu, wd, sx, sy, rx, ry, by, bx, xs, ys, part, got, relay, act, gu, gg,
    tab_s, tab_r, tx_s, tx_r, tc_s, tc_r, loc,
    sx_s, sx_r, sy_s, sy_r, bks_y, bkr_y, bks_x, bkr_x,
    rs_s, rs_r, ag_s, ag_r,
    fm_s, fm_r, fd_s, fd_r,
):
    d = lax.axis_index("dp")
    t = lax.axis_index("tensor")
    c = lax.axis_index("context")
    core = lax.rem(t, 2)
    py = (t // 2) * 2 + c // 4
    pz = lax.rem(c, 4)
    width = tx.shape[2]
    half = width // 2

    def offset(j):
        kpos, i = j // PER, lax.rem(j, PER)
        kk = lax.rem(2 + 2 * kpos + (kpos // 2) * 3, 4)
        z = lax.rem(i, 4)
        return i // 4, lax.rem(kk + 4 - z, 4), z

    def peer(j, sign):
        a, y, z = offset(j)
        if sign < 0:
            y, z = 4 - y, 4 - z
        y, z = lax.rem(py + y, 4), lax.rem(pz + z, 4)
        return (d, (y // 2) * 2 + lax.rem(core + a, 2), lax.rem(y, 2) * 4 + z)

    def ring(p):
        return (lax.rem(d + p, GROUPS), t, c)

    def remote(src, dst, s, r, dev):
        return pltpu.make_async_remote_copy(
            src_ref=src, dst_ref=dst, send_sem=s, recv_sem=r, device_id=dev, device_id_type=MESH
        )

    barrier = pltpu.get_barrier_semaphore()

    def greet(j, carry):
        @pl.when(j != SELF)
        def _():
            pl.semaphore_signal(barrier, inc=1, device_id=peer(j, 1), device_id_type=MESH)

        return carry

    lax.fori_loop(0, EXPERTS, greet, 0)
    for p in range(1, GROUPS):
        pl.semaphore_signal(barrier, inc=1, device_id=ring(p), device_id_type=MESH)

    e = lax.broadcasted_iota(jnp.int32, (EXPERTS, TOK), 0)
    e_core = (e >> 3) & 1
    e_y = (e >> 4) * 2 + ((e >> 2) & 1)
    e_z = e & 3
    oa = (e_core - core + 2) & 1
    oy = (e_y - py + 4) & 3
    oz = (e_z - pz + 4) & 3
    kk = (oy + oz) & 3
    kpos = jnp.where(kk == 2, 0, jnp.where(kk == 0, 1, jnp.where(kk == 1, 2, 3)))
    first_row = ((kpos * PER + oa * 4 + oz) * SLAB + d * CAP).astype(jnp.float32)
    e_f = e.astype(jnp.float32)
    tab = tab_ref[...]
    chosen0 = jnp.where(e_f == tab[0:1, :], 1.0, 0.0)
    chosen1 = jnp.where(e_f == tab[1:2, :], 1.0, 0.0)
    earlier = jnp.where(
        lax.broadcasted_iota(jnp.int32, (TOK, TOK), 0) < lax.broadcasted_iota(jnp.int32, (TOK, TOK), 1), 1.0, 0.0
    ).astype(jnp.bfloat16)
    before = dot((chosen0 + chosen1).astype(jnp.bfloat16), earlier)
    place = first_row + before
    key0 = jnp.sum(chosen0 * place, axis=0, keepdims=True)
    key1 = jnp.sum(chosen1 * place, axis=0, keepdims=True)
    tb[d] = jnp.concatenate([key0, key1, tab[2:4, :], jnp.zeros((4, TOK), jnp.float32)], axis=0)

    pl.semaphore_wait(barrier, EXPERTS - 1 + GROUPS - 1)

    def tables(p):
        return remote(tb.at[d], tb.at[d], tab_s.at[p - 1], tab_r.at[p - 1], ring(p))

    for p in range(1, GROUPS):
        tables(p).start()

    def columns(p):
        q = lax.rem(d + p, GROUPS)
        return pl.ds(pl.multiple_of(q * width, width), width)

    def dense(src, dst, s, r, p):
        return remote(src.at[:, columns(p)], dst.at[d], s.at[p - 1], r.at[p - 1], ring(p))

    own_tx = pltpu.make_async_copy(tokens.at[:, columns(0)], tx.at[d], loc.at[0])
    own_tc = pltpu.make_async_copy(cotangent.at[:, columns(0)], tc.at[d], loc.at[1])
    for p in range(1, GROUPS):
        dense(tokens, tx, tx_s, tx_r, p).start()
    own_tx.start()
    for p in range(1, GROUPS):
        dense(cotangent, tc, tc_s, tc_r, p).start()
    own_tc.start()
    weights = [
        pltpu.make_async_copy(w_gate.at[0], wg, loc.at[2]),
        pltpu.make_async_copy(w_up.at[0], wu, loc.at[3]),
        pltpu.make_async_copy(w_down.at[0], wd, loc.at[4]),
    ]
    for w in weights:
        w.start()

    for p in range(1, GROUPS):
        tables(p).wait()

    def halves(value):
        return [value[:, h * half : (h + 1) * half].reshape(PER, SLAB, half) for h in range(2)]

    def to_slabs(buf, k, value):
        for h, v in enumerate(halves(value)):
            buf[pl.ds(k * PER, PER), h * SLAB : (h + 1) * SLAB, :] = v.astype(jnp.bfloat16)

    def from_slabs(buf, k, h):
        v = buf[pl.ds(k * PER, PER), h * SLAB : (h + 1) * SLAB, :].astype(jnp.float32)
        return v.reshape(ROWS, half).astype(jnp.bfloat16)

    def slab_copy(src, dst, s, r, j, sign):
        return remote(src.at[j], dst.at[j], s.at[j // PER], r.at[j // PER], peer(j, sign))

    def each_slot(k, act_on):
        def body(i, carry):
            j = k * PER + i

            @pl.when(j != SELF)
            def _():
                act_on(j)

            return carry

        lax.fori_loop(0, PER, body, 0)

    def send_slabs(src, dst, s, r, k, sign):
        each_slot(k, lambda j: slab_copy(src, dst, s, r, j, sign).start())

        @pl.when(k == SELF // PER)
        def _():
            dst[SELF] = src[SELF]

    def await_bytes(buf, sem, k):
        @pl.when(k == SELF // PER)
        def _():
            ref = buf.at[pl.ds(SELF + 1, PER - 1)]
            pltpu.make_async_copy(ref, ref, sem.at[k]).wait()

        @pl.when(k != SELF // PER)
        def _():
            ref = buf.at[pl.ds(k * PER, PER)]
            pltpu.make_async_copy(ref, ref, sem.at[k]).wait()

    def await_slabs(src, dst, s, r, k, sign):
        await_bytes(dst, r, k)

    def await_sent(src, dst, s, r, k, sign):
        await_bytes(src, s, k)

    for p in range(1, GROUPS):
        dense(tokens, tx, tx_s, tx_r, p).wait()
    own_tx.wait()

    def send_x(k, carry):
        row = (lax.broadcasted_iota(jnp.int32, (ROWS, TOK), 0) + k * ROWS).astype(jnp.float32)
        for g in range(GROUPS):
            info = tb[g]
            hit0, hit1 = row == info[0:1, :], row == info[1:2, :]
            cols = slice(g * TOK, (g + 1) * TOK)
            oh[k, :, cols] = jnp.where(hit0 | hit1, 1.0, 0.0).astype(jnp.bfloat16)
            og[k, :, cols] = jnp.where(hit0, info[2:3, :], jnp.where(hit1, info[3:4, :], 0.0))
        to_slabs(sx, k, dot(oh[k], tx[...].reshape(GROUPS * TOK, width)))
        send_slabs(sx, rx, sx_s, sx_r, k, 1)
        return carry

    lax.fori_loop(0, CHUNKS, send_x, 0)

    def send_dy(k):
        weight = jnp.sum(og[k], axis=1, keepdims=True)
        to_slabs(sy, k, dot(oh[k], tc[...].reshape(GROUPS * TOK, width)) * weight)
        send_slabs(sy, ry, sy_s, sy_r, k, 1)

    def await_cot():
        for p in range(1, GROUPS):
            dense(cotangent, tc, tc_s, tc_r, p).wait()
        own_tc.wait()

    for w in weights:
        w.wait()

    def way(k, q, mixed_q):
        if q == mixed_q:
            return 1 + 2 * lax.rem(k, 2)
        return 1 if q == min({0, 1, 2} - {mixed_q}) else 3

    def towards(n):
        return lax.rem(d + n, GROUPS)

    def rs(k, q, kind):
        w = way(k, q, 2)
        s, r = rs_s.at[0], rs_r.at[k, q, min(kind, 1)]
        if kind == 0:
            return remote(part.at[k, towards(2), q], relay.at[k, q], s, r, ring(w))
        if kind == 1:
            return remote(part.at[k, towards(4 - w), q], got.at[k, q, 0], s, r, ring(4 - w))
        return remote(part.at[k, towards(w), q], got.at[k, q, 1], s, r, ring(w))

    def rs_start(k, q):
        rs(k, q, 0).start()
        rs(k, q, 1).start()

    def rs_add(k, q):
        rs(k, q, 0).wait_recv()
        o = towards(way(k, q, 2))
        part[k, o, q] = (part[k, o, q].astype(jnp.float32) + relay[k, q].astype(jnp.float32)).astype(jnp.bfloat16)
        rs(k, q, 2).start()

    def rs_total(k, q):
        pltpu.make_async_copy(got.at[k, q], got.at[k, q], rs_r.at[k, q, 1]).wait()
        total = part[k, d, q].astype(jnp.float32)
        return total + got[k, q, 0].astype(jnp.float32) + got[k, q, 1].astype(jnp.float32)

    def ag(k, q, kind):
        w = way(k, q, 0)
        s, r = ag_s.at[0], ag_r.at[k, q, min(kind, 1)]
        o = d if kind < 2 else towards(4 - w)
        return remote(act.at[q, k, o], act.at[q, k, o], s, r, ring(w if kind != 1 else 4 - w))

    def ag_start(k, q):
        ag(k, q, 0).start()
        ag(k, q, 1).start()

    def ag_forward(k, q):
        ag(k, q, 0).wait_recv()
        ag(k, q, 2).start()

    def ag_whole(k, q):
        two = act.at[q, k, pl.ds(0, 2)]
        pltpu.make_async_copy(two, two, ag_r.at[k, q, 1]).wait()
        return act[q, k].reshape(ROWS, act.shape[4])

    def partial_sums(k, q, value):
        part[k, :, q] = value.astype(jnp.bfloat16).reshape(GROUPS, OWN, value.shape[1])

    def first(k):
        await_slabs(sx, rx, sx_s, sx_r, k, 1)
        for h in range(2):
            xs[k, :, h * half : (h + 1) * half] = from_slabs(rx, k, h)
        partial_sums(k, 0, dot(xs[k], wg[...]))
        rs_start(k, 0)
        partial_sums(k, 1, dot(xs[k], wu[...]))
        rs_start(k, 1)

    def first_add(k):
        rs_add(k, 0)
        rs_add(k, 1)

    def first_total(k):
        gate_h, up_h = rs_total(k, 0), rs_total(k, 1)
        gu[k, 0] = gate_h
        gu[k, 1] = up_h
        act[0, k, d] = (gate_h * jax.nn.sigmoid(gate_h) * up_h).astype(jnp.bfloat16)
        ag_start(k, 0)

    def second(k):
        await_slabs(sy, ry, sy_s, sy_r, k, 1)
        for h in range(2):
            ys[k, :, h * half : (h + 1) * half] = from_slabs(ry, k, h)
        partial_sums(k, 2, lax.dot_general(ys[k], wd[...], NT, preferred_element_type=jnp.float32))
        rs_start(k, 2)

    def second_total(k):
        d_h = rs_total(k, 2)
        gate_h, up_h = gu[k, 0], gu[k, 1]
        sigma = jax.nn.sigmoid(gate_h)
        act[1, k, d] = (d_h * up_h * sigma * (1.0 + gate_h * (1.0 - sigma))).astype(jnp.bfloat16)
        ag_start(k, 1)
        act[2, k, d] = (d_h * (gate_h * sigma)).astype(jnp.bfloat16)
        ag_start(k, 2)

    def second_forward(k):
        ag_forward(k, 1)
        ag_forward(k, 2)

    def send_y(k):
        y = dot(ag_whole(k, 0), wd[...])
        await_sent(sx, rx, sx_s, sx_r, k, 1)
        to_slabs(sx, k, y)
        send_slabs(sx, by, bks_y, bkr_y, k, -1)

    def send_dx(k):
        dx = lax.dot_general(ag_whole(k, 1), wg[...], NT, preferred_element_type=jnp.float32)
        dx += lax.dot_general(ag_whole(k, 2), wu[...], NT, preferred_element_type=jnp.float32)
        await_sent(sy, ry, sy_s, sy_r, k, 1)
        to_slabs(sy, k, dx)
        send_slabs(sy, bx, bks_x, bkr_x, k, -1)

    def final(src, dst, s, r, p, h):
        cols = pl.ds(pl.multiple_of(d * width + h * half, half), half)
        out = src.at[lax.rem(d + p, GROUPS), :, pl.ds(h * half, half)]
        return remote(out, dst.at[:, cols], s.at[p - 1, h], r.at[p - 1, h], ring(p))

    def combine(buf, arrived, matrix, stage, dst, s, r):
        for h in range(2):
            total = jnp.zeros((GROUPS * TOK, half), jnp.float32)
            for k in range(CHUNKS):
                if h == 0:
                    await_bytes(buf, arrived, jnp.int32(k))
                total += lax.dot_general(matrix(k), from_slabs(buf, k, h), TN, preferred_element_type=jnp.float32)
            stage[:, :, h * half : (h + 1) * half] = total.astype(jnp.bfloat16).reshape(GROUPS, TOK, half)
            for p in (2, 1, 3):
                final(stage, dst, s, r, p, h).start()

    def own_out(src, dst, sem):
        return pltpu.make_async_copy(src.at[d], dst.at[:, columns(0)], sem)

    def finish_y():
        combine(by, bkr_y, lambda k: og[k].astype(jnp.bfloat16), tx, mixed, fm_s, fm_r)
        own_out(tx, mixed, loc.at[0]).start()

    stages = (
        (0, first),
        (DY_AT, send_dy),
        (1, first_add),
        (2, first_total),
        (3, lambda k: ag_forward(k, 0)),
        (4, second),
        (4, send_y),
        (5, lambda k: rs_add(k, 2)),
        (6, second_total),
        (7, second_forward),
        (8, send_dx),
    )
    last = CHUNKS - 1 + max(lag for lag, _ in stages)

    def step(now, carry):
        @pl.when(now == DY_AT)
        def _():
            await_cot()

        @pl.when(now == last)
        def _():
            finish_y()

        for lag, stage in stages:
            pl.when((now >= lag) & (now < lag + CHUNKS))(functools.partial(stage, now - lag))
        return carry

    lax.fori_loop(0, last + 1, step, 0)

    block = 256

    def all_rows(q):
        return act[q].reshape(CHUNKS * ROWS, act.shape[4])

    def weight_grads(b, carry):
        cols = pl.ds(pl.multiple_of(b * block, block), block)
        x = xs[:, :, cols].reshape(CHUNKS * ROWS, block)
        gg[0, cols, :] = lax.dot_general(x, all_rows(1), TN, preferred_element_type=jnp.float32).astype(jnp.bfloat16)
        gg[1, cols, :] = lax.dot_general(x, all_rows(2), TN, preferred_element_type=jnp.float32).astype(jnp.bfloat16)
        return carry

    lax.fori_loop(0, width // block, weight_grads, 0)
    outs = [
        pltpu.make_async_copy(gg.at[0], g_gate.at[0], loc.at[2]),
        pltpu.make_async_copy(gg.at[1], g_up.at[0], loc.at[3]),
        pltpu.make_async_copy(wd, g_down.at[0], loc.at[4]),
    ]
    outs[0].start()
    outs[1].start()

    def down_grads(b, carry):
        cols = pl.ds(pl.multiple_of(b * block, block), block)
        dy = ys[:, :, cols].reshape(CHUNKS * ROWS, block)
        wd[:, cols] = lax.dot_general(all_rows(0), dy, TN, preferred_element_type=jnp.float32).astype(jnp.bfloat16)
        return carry

    lax.fori_loop(0, width // block, down_grads, 0)
    outs[2].start()

    combine(bx, bkr_x, lambda k: oh[k], tc, d_tokens, fd_s, fd_r)
    own_out(tc, d_tokens, loc.at[1]).start()
    for p in range(1, GROUPS):
        for h in range(2):
            final(tx, mixed, fm_s, fm_r, p, h).wait()
            final(tc, d_tokens, fd_s, fd_r, p, h).wait()
    own_out(tx, mixed, loc.at[0]).wait()
    own_out(tc, d_tokens, loc.at[1]).wait()
    for o in outs:
        o.wait()

    def back_sent(k, carry):
        await_bytes(sx, bks_y, k)
        await_bytes(sy, bks_x, k)
        return carry

    lax.fori_loop(0, CHUNKS, back_sent, 0)
    sums, gathers = part.at[pl.ds(0, 3)], act.at[:, pl.ds(0, 3)]
    pltpu.make_async_copy(sums, sums, rs_s.at[0]).wait()
    pltpu.make_async_copy(gathers, gathers, ag_s.at[0]).wait()


def publish(*refs):
    sources, targets, held, (come, go) = refs[:5], refs[5:10], refs[10:15], refs[15:]
    reads = [pltpu.make_async_copy(sources[i], held[i], come.at[i]) for i in range(5)]
    writes = [pltpu.make_async_copy(held[i], targets[i], go.at[i]) for i in range(5)]
    for read in reads:
        read.start()
    for read, write in zip(reads, writes):
        read.wait()
        write.start()
    for write in writes:
        write.wait()


def shards(tokens, routes, gates, cotangent, w_gate, w_up, w_down):
    tok, full = tokens.shape
    ff = w_gate.shape[2]
    width = full // GROUPS
    bf16, f32 = jnp.bfloat16, jnp.float32
    tab = jnp.concatenate([routes.astype(f32), gates], axis=1).T
    hbm = pl.BlockSpec(memory_space=pl.ANY)
    vmem = pl.BlockSpec(memory_space=pltpu.VMEM)
    slabs = pltpu.VMEM((EXPERTS, 2 * SLAB, width // 2), bf16)
    sem = pltpu.SemaphoreType.DMA
    results = pl.pallas_call(
        kernel,
        out_shape=(
            jax.ShapeDtypeStruct(tokens.shape, bf16),
            jax.ShapeDtypeStruct(tokens.shape, bf16),
            jax.ShapeDtypeStruct(w_gate.shape, bf16),
            jax.ShapeDtypeStruct(w_up.shape, bf16),
            jax.ShapeDtypeStruct(w_down.shape, bf16),
        ),
        in_specs=[vmem] + [hbm] * 5,
        out_specs=(hbm,) * 5,
        scratch_shapes=[
            pltpu.VMEM((GROUPS, 8, tok), f32),
            pltpu.VMEM((GROUPS, tok, width), bf16),
            pltpu.VMEM((GROUPS, tok, width), bf16),
            pltpu.VMEM((CHUNKS, ROWS, GROUPS * tok), bf16),
            pltpu.VMEM((CHUNKS, ROWS, GROUPS * tok), f32),
            pltpu.VMEM((width, ff), bf16),
            pltpu.VMEM((width, ff), bf16),
            pltpu.VMEM((ff, width), bf16),
            slabs, slabs, slabs, slabs, slabs, slabs,
            pltpu.VMEM((CHUNKS, ROWS, width), bf16),
            pltpu.VMEM((CHUNKS, ROWS, width), bf16),
            pltpu.VMEM((CHUNKS, GROUPS, 3, OWN, ff), bf16),
            pltpu.VMEM((CHUNKS, 3, 2, OWN, ff), bf16),
            pltpu.VMEM((CHUNKS, 3, OWN, ff), bf16),
            pltpu.VMEM((3, CHUNKS, GROUPS, OWN, ff), bf16),
            pltpu.VMEM((CHUNKS, 2, OWN, ff), f32),
            pltpu.VMEM((2, width, ff), bf16),
            sem((3,)), sem((3,)), sem((3,)), sem((3,)), sem((3,)), sem((3,)), sem((5,)),
        ]
        + [sem((CHUNKS,))] * 8
        + [sem((1,)), sem((CHUNKS, 3, 2)), sem((1,)), sem((CHUNKS, 3, 2))]
        + [sem((3, 2))] * 4,
        compiler_params=pltpu.CompilerParams(
            collective_id=0, has_side_effects=True, vmem_limit_bytes=62 * 2**20
        ),
        cost_estimate=pl.CostEstimate(flops=24 * 10**9, bytes_accessed=14 * 10**6, transcendentals=500000),
    )(tab, tokens, cotangent, w_gate, w_up, w_down)
    return pl.pallas_call(
        publish,
        out_shape=[jax.ShapeDtypeStruct(r.shape, r.dtype) for r in results],
        in_specs=[hbm] * 5,
        out_specs=[hbm] * 5,
        scratch_shapes=[pltpu.VMEM(r.shape, r.dtype) for r in results] + [sem((5,)), sem((5,))],
        compiler_params=pltpu.CompilerParams(vmem_limit_bytes=62 * 2**20),
    )(*results)


def solution(mesh):
    placed = (
        P(("dp", "tensor", "context"), None),
        P(("dp", "tensor", "context"), None),
        P(("dp", "tensor", "context"), None),
        P(("dp", "tensor", "context"), None),
        P(("tensor", "context"), "dp", None),
        P(("tensor", "context"), "dp", None),
        P(("tensor", "context"), None, "dp"),
    )
    return jax.shard_map(
        shards,
        mesh=mesh,
        in_specs=placed,
        out_specs=(
            P(("dp", "tensor", "context"), None),
            P(("dp", "tensor", "context"), None),
            P(("tensor", "context"), "dp", None),
            P(("tensor", "context"), "dp", None),
            P(("tensor", "context"), None, "dp"),
        ),
        check_vma=False,
    )
```

```python
import functools

import jax
import jax.numpy as jnp
from jax import lax
from jax.experimental import pallas as pl
from jax.experimental.pallas import tpu as pltpu
from jax.sharding import PartitionSpec as P

MESH = pl.DeviceIdType.MESH
DY_AT = 1
GROUPS = 4
EXPERTS = 32
CAP = 10
TOK = 128
SLAB = GROUPS * CAP
CHUNKS = 4
PER = EXPERTS // CHUNKS
ROWS = PER * SLAB
OWN = ROWS // GROUPS
SELF = 8

NT = (((1,), (1,)), ((), ()))
TN = (((0,), (0,)), ((), ()))


def dot(a, b):
    return jnp.dot(a, b, preferred_element_type=jnp.float32)


def kernel(
    tab_ref, tokens, cotangent, w_gate, w_up, w_down,
    mixed, d_tokens, g_gate, g_up, g_down,
    tb, tx, tc, oh, og, wg, wu, wd, sx, sy, rx, ry, by, bx, xs, ys, part, got, relay, act, gu, gg,
    tab_s, tab_r, tx_s, tx_r, tc_s, tc_r, loc,
    sx_s, sx_r, sy_s, sy_r, bks_y, bkr_y, bks_x, bkr_x,
    rs_s, rs_r, ag_s, ag_r,
    fm_s, fm_r, fd_s, fd_r,
):
    d = lax.axis_index("dp")
    t = lax.axis_index("tensor")
    c = lax.axis_index("context")
    core = lax.rem(t, 2)
    py = (t // 2) * 2 + c // 4
    pz = lax.rem(c, 4)
    width = tx.shape[2]
    half = width // 2

    def offset(j):
        kpos, i = j // PER, lax.rem(j, PER)
        kk = lax.rem(2 + 2 * kpos + (kpos // 2) * 3, 4)
        z = lax.rem(i, 4)
        return i // 4, lax.rem(kk + 4 - z, 4), z

    def peer(j, sign):
        a, y, z = offset(j)
        if sign < 0:
            y, z = 4 - y, 4 - z
        y, z = lax.rem(py + y, 4), lax.rem(pz + z, 4)
        return (d, (y // 2) * 2 + lax.rem(core + a, 2), lax.rem(y, 2) * 4 + z)

    def ring(p):
        return (lax.rem(d + p, GROUPS), t, c)

    def remote(src, dst, s, r, dev):
        return pltpu.make_async_remote_copy(
            src_ref=src, dst_ref=dst, send_sem=s, recv_sem=r, device_id=dev, device_id_type=MESH
        )

    barrier = pltpu.get_barrier_semaphore()

    def greet(j, carry):
        @pl.when(j != SELF)
        def _():
            pl.semaphore_signal(barrier, inc=1, device_id=peer(j, 1), device_id_type=MESH)

        return carry

    lax.fori_loop(0, EXPERTS, greet, 0)
    for p in range(1, GROUPS):
        pl.semaphore_signal(barrier, inc=1, device_id=ring(p), device_id_type=MESH)

    e = lax.broadcasted_iota(jnp.int32, (EXPERTS, TOK), 0)
    e_core = (e >> 3) & 1
    e_y = (e >> 4) * 2 + ((e >> 2) & 1)
    e_z = e & 3
    oa = (e_core - core + 2) & 1
    oy = (e_y - py + 4) & 3
    oz = (e_z - pz + 4) & 3
    kk = (oy + oz) & 3
    kpos = jnp.where(kk == 2, 0, jnp.where(kk == 0, 1, jnp.where(kk == 1, 2, 3)))
    first_row = ((kpos * PER + oa * 4 + oz) * SLAB + d * CAP).astype(jnp.float32)
    e_f = e.astype(jnp.float32)
    tab = tab_ref[...]
    chosen0 = jnp.where(e_f == tab[0:1, :], 1.0, 0.0)
    chosen1 = jnp.where(e_f == tab[1:2, :], 1.0, 0.0)
    earlier = jnp.where(
        lax.broadcasted_iota(jnp.int32, (TOK, TOK), 0) < lax.broadcasted_iota(jnp.int32, (TOK, TOK), 1), 1.0, 0.0
    ).astype(jnp.bfloat16)
    before = dot((chosen0 + chosen1).astype(jnp.bfloat16), earlier)
    place = first_row + before
    key0 = jnp.sum(chosen0 * place, axis=0, keepdims=True)
    key1 = jnp.sum(chosen1 * place, axis=0, keepdims=True)
    tb[d] = jnp.concatenate([key0, key1, tab[2:4, :], jnp.zeros((4, TOK), jnp.float32)], axis=0)

    pl.semaphore_wait(barrier, EXPERTS - 1 + GROUPS - 1)

    def tables(p):
        return remote(tb.at[d], tb.at[d], tab_s.at[p - 1], tab_r.at[p - 1], ring(p))

    for p in range(1, GROUPS):
        tables(p).start()

    def columns(p):
        q = lax.rem(d + p, GROUPS)
        return pl.ds(pl.multiple_of(q * width, width), width)

    def dense(src, dst, s, r, p):
        return remote(src.at[:, columns(p)], dst.at[d], s.at[p - 1], r.at[p - 1], ring(p))

    own_tx = pltpu.make_async_copy(tokens.at[:, columns(0)], tx.at[d], loc.at[0])
    own_tc = pltpu.make_async_copy(cotangent.at[:, columns(0)], tc.at[d], loc.at[1])
    own_tx.start()
    for p in (2, 1, 3):
        dense(tokens, tx, tx_s, tx_r, p).start()
    for p in range(1, GROUPS):
        dense(cotangent, tc, tc_s, tc_r, p).start()
    own_tc.start()
    weights = [
        pltpu.make_async_copy(w_gate.at[0], wg, loc.at[2]),
        pltpu.make_async_copy(w_up.at[0], wu, loc.at[3]),
        pltpu.make_async_copy(w_down.at[0], wd, loc.at[4]),
    ]
    for w in weights:
        w.start()

    for p in range(1, GROUPS):
        tables(p).wait()

    def halves(value):
        return [value[:, h * half : (h + 1) * half].reshape(PER, SLAB, half) for h in range(2)]

    def to_slabs(buf, k, value):
        for h, v in enumerate(halves(value)):
            buf[pl.ds(k * PER, PER), h * SLAB : (h + 1) * SLAB, :] = v.astype(jnp.bfloat16)

    def from_slabs(buf, k, h):
        v = buf[pl.ds(k * PER, PER), h * SLAB : (h + 1) * SLAB, :].astype(jnp.float32)
        return v.reshape(ROWS, half).astype(jnp.bfloat16)

    def slab_copy(src, dst, s, r, j, sign):
        return remote(src.at[j], dst.at[j], s.at[j // PER], r.at[j // PER], peer(j, sign))

    def each_slot(k, act_on):
        def body(i, carry):
            j = k * PER + i

            @pl.when(j != SELF)
            def _():
                act_on(j)

            return carry

        lax.fori_loop(0, PER, body, 0)

    def send_slabs(src, dst, s, r, k, sign):
        each_slot(k, lambda j: slab_copy(src, dst, s, r, j, sign).start())

        @pl.when(k == SELF // PER)
        def _():
            dst[SELF] = src[SELF]

    def await_bytes(buf, sem, k):
        @pl.when(k == SELF // PER)
        def _():
            ref = buf.at[pl.ds(SELF + 1, PER - 1)]
            pltpu.make_async_copy(ref, ref, sem.at[k]).wait()

        @pl.when(k != SELF // PER)
        def _():
            ref = buf.at[pl.ds(k * PER, PER)]
            pltpu.make_async_copy(ref, ref, sem.at[k]).wait()

    def await_slabs(src, dst, s, r, k, sign):
        await_bytes(dst, r, k)

    def await_sent(src, dst, s, r, k, sign):
        await_bytes(src, s, k)

    for p in range(1, GROUPS):
        dense(tokens, tx, tx_s, tx_r, p).wait()
    own_tx.wait()

    def send_x(k, carry):
        row = (lax.broadcasted_iota(jnp.int32, (ROWS, TOK), 0) + k * ROWS).astype(jnp.float32)
        for g in range(GROUPS):
            info = tb[g]
            hit0, hit1 = row == info[0:1, :], row == info[1:2, :]
            cols = slice(g * TOK, (g + 1) * TOK)
            oh[k, :, cols] = jnp.where(hit0 | hit1, 1.0, 0.0).astype(jnp.bfloat16)
            og[k, :, cols] = jnp.where(hit0, info[2:3, :], jnp.where(hit1, info[3:4, :], 0.0))
        to_slabs(sx, k, dot(oh[k], tx[...].reshape(GROUPS * TOK, width)))
        send_slabs(sx, rx, sx_s, sx_r, k, 1)
        return carry

    lax.fori_loop(0, CHUNKS, send_x, 0)

    def send_dy(k):
        weight = jnp.sum(og[k], axis=1, keepdims=True)
        to_slabs(sy, k, dot(oh[k], tc[...].reshape(GROUPS * TOK, width)) * weight)
        send_slabs(sy, ry, sy_s, sy_r, k, 1)

    def await_cot():
        for p in range(1, GROUPS):
            dense(cotangent, tc, tc_s, tc_r, p).wait()
        own_tc.wait()

    for w in weights:
        w.wait()

    def way(k, q, mixed_q):
        if q == mixed_q:
            return 1 + 2 * lax.rem(k, 2)
        return 1 if q == min({0, 1, 2} - {mixed_q}) else 3

    def towards(n):
        return lax.rem(d + n, GROUPS)

    def rs(k, q, kind):
        w = way(k, q, 2)
        s, r = rs_s.at[0], rs_r.at[k, q, min(kind, 1)]
        if kind == 0:
            return remote(part.at[k, towards(2), q], relay.at[k, q], s, r, ring(w))
        if kind == 1:
            return remote(part.at[k, towards(4 - w), q], got.at[k, q, 0], s, r, ring(4 - w))
        return remote(part.at[k, towards(w), q], got.at[k, q, 1], s, r, ring(w))

    def rs_start(k, q):
        rs(k, q, 0).start()
        rs(k, q, 1).start()

    def rs_add(k, q):
        rs(k, q, 0).wait_recv()
        o = towards(way(k, q, 2))
        part[k, o, q] = (part[k, o, q].astype(jnp.float32) + relay[k, q].astype(jnp.float32)).astype(jnp.bfloat16)
        rs(k, q, 2).start()

    def rs_total(k, q):
        pltpu.make_async_copy(got.at[k, q], got.at[k, q], rs_r.at[k, q, 1]).wait()
        total = part[k, d, q].astype(jnp.float32)
        return total + got[k, q, 0].astype(jnp.float32) + got[k, q, 1].astype(jnp.float32)

    def ag(k, q, kind):
        w = way(k, q, 0)
        s, r = ag_s.at[0], ag_r.at[k, q, min(kind, 1)]
        o = d if kind < 2 else towards(4 - w)
        return remote(act.at[q, k, o], act.at[q, k, o], s, r, ring(w if kind != 1 else 4 - w))

    def ag_start(k, q):
        ag(k, q, 0).start()
        ag(k, q, 1).start()

    def ag_forward(k, q):
        ag(k, q, 0).wait_recv()
        ag(k, q, 2).start()

    def ag_whole(k, q):
        two = act.at[q, k, pl.ds(0, 2)]
        pltpu.make_async_copy(two, two, ag_r.at[k, q, 1]).wait()
        return act[q, k].reshape(ROWS, act.shape[4])

    def partial_sums(k, q, value):
        part[k, :, q] = value.astype(jnp.bfloat16).reshape(GROUPS, OWN, value.shape[1])

    def first(k):
        await_slabs(sx, rx, sx_s, sx_r, k, 1)
        for h in range(2):
            xs[k, :, h * half : (h + 1) * half] = from_slabs(rx, k, h)
        partial_sums(k, 0, dot(xs[k], wg[...]))
        rs_start(k, 0)
        partial_sums(k, 1, dot(xs[k], wu[...]))
        rs_start(k, 1)

    def first_add(k):
        rs_add(k, 0)
        rs_add(k, 1)

    def first_total(k):
        gate_h, up_h = rs_total(k, 0), rs_total(k, 1)
        gu[k, 0] = gate_h
        gu[k, 1] = up_h
        act[0, k, d] = (gate_h * jax.nn.sigmoid(gate_h) * up_h).astype(jnp.bfloat16)
        ag_start(k, 0)

    def second(k):
        await_slabs(sy, ry, sy_s, sy_r, k, 1)
        for h in range(2):
            ys[k, :, h * half : (h + 1) * half] = from_slabs(ry, k, h)
        partial_sums(k, 2, lax.dot_general(ys[k], wd[...], NT, preferred_element_type=jnp.float32))
        rs_start(k, 2)

    def second_total(k):
        d_h = rs_total(k, 2)
        gate_h, up_h = gu[k, 0], gu[k, 1]
        sigma = jax.nn.sigmoid(gate_h)
        act[1, k, d] = (d_h * up_h * sigma * (1.0 + gate_h * (1.0 - sigma))).astype(jnp.bfloat16)
        ag_start(k, 1)
        act[2, k, d] = (d_h * (gate_h * sigma)).astype(jnp.bfloat16)
        ag_start(k, 2)

    def second_forward(k):
        ag_forward(k, 1)
        ag_forward(k, 2)

    def send_y(k):
        y = dot(ag_whole(k, 0), wd[...])
        await_sent(sx, rx, sx_s, sx_r, k, 1)
        to_slabs(sx, k, y)
        send_slabs(sx, by, bks_y, bkr_y, k, -1)

    def send_dx(k):
        dx = lax.dot_general(ag_whole(k, 1), wg[...], NT, preferred_element_type=jnp.float32)
        dx += lax.dot_general(ag_whole(k, 2), wu[...], NT, preferred_element_type=jnp.float32)
        await_sent(sy, ry, sy_s, sy_r, k, 1)
        to_slabs(sy, k, dx)
        send_slabs(sy, bx, bks_x, bkr_x, k, -1)

    def final(src, dst, s, r, p, h):
        cols = pl.ds(pl.multiple_of(d * width + h * half, half), half)
        out = src.at[lax.rem(d + p, GROUPS), :, pl.ds(h * half, half)]
        return remote(out, dst.at[:, cols], s.at[p - 1, h], r.at[p - 1, h], ring(p))

    def combine(buf, arrived, matrix, stage, dst, s, r):
        for h in range(2):
            total = jnp.zeros((GROUPS * TOK, half), jnp.float32)
            for k in range(CHUNKS):
                if h == 0:
                    await_bytes(buf, arrived, jnp.int32(k))
                total += lax.dot_general(matrix(k), from_slabs(buf, k, h), TN, preferred_element_type=jnp.float32)
            stage[:, :, h * half : (h + 1) * half] = total.astype(jnp.bfloat16).reshape(GROUPS, TOK, half)
            for p in (2, 1, 3):
                final(stage, dst, s, r, p, h).start()

    def own_out(src, dst, sem):
        return pltpu.make_async_copy(src.at[d], dst.at[:, columns(0)], sem)

    def finish_y():
        combine(by, bkr_y, lambda k: og[k].astype(jnp.bfloat16), tx, mixed, fm_s, fm_r)
        own_out(tx, mixed, loc.at[0]).start()

    stages = (
        (0, first),
        (DY_AT, send_dy),
        (1, first_add),
        (2, first_total),
        (3, lambda k: ag_forward(k, 0)),
        (4, second),
        (4, send_y),
        (5, lambda k: rs_add(k, 2)),
        (6, second_total),
        (7, second_forward),
        (8, send_dx),
    )
    last = CHUNKS - 1 + max(lag for lag, _ in stages)

    def step(now, carry):
        @pl.when(now == DY_AT)
        def _():
            await_cot()

        @pl.when(now == last)
        def _():
            finish_y()

        for lag, stage in stages:
            pl.when((now >= lag) & (now < lag + CHUNKS))(functools.partial(stage, now - lag))
        return carry

    lax.fori_loop(0, last + 1, step, 0)

    block = 256

    def all_rows(q):
        return act[q].reshape(CHUNKS * ROWS, act.shape[4])

    outs = [
        pltpu.make_async_copy(gg.at[0], g_gate.at[0], loc.at[2]),
        pltpu.make_async_copy(gg.at[1], g_up.at[0], loc.at[3]),
        pltpu.make_async_copy(wd, g_down.at[0], loc.at[4]),
    ]
    def down_grads(b, carry):
        cols = pl.ds(pl.multiple_of(b * block, block), block)
        dy = ys[:, :, cols].reshape(CHUNKS * ROWS, block)
        wd[:, cols] = lax.dot_general(all_rows(0), dy, TN, preferred_element_type=jnp.float32).astype(jnp.bfloat16)
        return carry

    lax.fori_loop(0, width // block, down_grads, 0)
    outs[2].start()

    combine(bx, bkr_x, lambda k: oh[k], tc, d_tokens, fd_s, fd_r)
    own_out(tc, d_tokens, loc.at[1]).start()
    def weight_grads(b, carry):
        cols = pl.ds(pl.multiple_of(b * block, block), block)
        x = xs[:, :, cols].reshape(CHUNKS * ROWS, block)
        gg[0, cols, :] = lax.dot_general(x, all_rows(1), TN, preferred_element_type=jnp.float32).astype(jnp.bfloat16)
        gg[1, cols, :] = lax.dot_general(x, all_rows(2), TN, preferred_element_type=jnp.float32).astype(jnp.bfloat16)
        return carry

    lax.fori_loop(0, width // block, weight_grads, 0)
    outs[0].start()
    outs[1].start()
    for p in range(1, GROUPS):
        for h in range(2):
            final(tx, mixed, fm_s, fm_r, p, h).wait()
            final(tc, d_tokens, fd_s, fd_r, p, h).wait()
    own_out(tx, mixed, loc.at[0]).wait()
    own_out(tc, d_tokens, loc.at[1]).wait()
    for o in outs:
        o.wait()

    def back_sent(k, carry):
        await_bytes(sx, bks_y, k)
        await_bytes(sy, bks_x, k)
        return carry

    lax.fori_loop(0, CHUNKS, back_sent, 0)
    sums, gathers = part.at[pl.ds(0, 3)], act.at[:, pl.ds(0, 3)]
    pltpu.make_async_copy(sums, sums, rs_s.at[0]).wait()
    pltpu.make_async_copy(gathers, gathers, ag_s.at[0]).wait()


def publish(*refs):
    sources, targets, held, (come, go) = refs[:5], refs[5:10], refs[10:15], refs[15:]
    reads = [pltpu.make_async_copy(sources[i], held[i], come.at[i]) for i in range(5)]
    writes = [pltpu.make_async_copy(held[i], targets[i], go.at[i]) for i in range(5)]
    for read in reads:
        read.start()
    for read, write in zip(reads, writes):
        read.wait()
        write.start()
    for write in writes:
        write.wait()


def shards(tokens, routes, gates, cotangent, w_gate, w_up, w_down):
    tok, full = tokens.shape
    ff = w_gate.shape[2]
    width = full // GROUPS
    bf16, f32 = jnp.bfloat16, jnp.float32
    tab = jnp.concatenate([routes.astype(f32), gates], axis=1).T
    hbm = pl.BlockSpec(memory_space=pl.ANY)
    vmem = pl.BlockSpec(memory_space=pltpu.VMEM)
    slabs = pltpu.VMEM((EXPERTS, 2 * SLAB, width // 2), bf16)
    sem = pltpu.SemaphoreType.DMA
    results = pl.pallas_call(
        kernel,
        out_shape=(
            jax.ShapeDtypeStruct(tokens.shape, bf16),
            jax.ShapeDtypeStruct(tokens.shape, bf16),
            jax.ShapeDtypeStruct(w_gate.shape, bf16),
            jax.ShapeDtypeStruct(w_up.shape, bf16),
            jax.ShapeDtypeStruct(w_down.shape, bf16),
        ),
        in_specs=[vmem] + [hbm] * 5,
        out_specs=(hbm,) * 5,
        scratch_shapes=[
            pltpu.VMEM((GROUPS, 8, tok), f32),
            pltpu.VMEM((GROUPS, tok, width), bf16),
            pltpu.VMEM((GROUPS, tok, width), bf16),
            pltpu.VMEM((CHUNKS, ROWS, GROUPS * tok), bf16),
            pltpu.VMEM((CHUNKS, ROWS, GROUPS * tok), f32),
            pltpu.VMEM((width, ff), bf16),
            pltpu.VMEM((width, ff), bf16),
            pltpu.VMEM((ff, width), bf16),
            slabs, slabs, slabs, slabs, slabs, slabs,
            pltpu.VMEM((CHUNKS, ROWS, width), bf16),
            pltpu.VMEM((CHUNKS, ROWS, width), bf16),
            pltpu.VMEM((CHUNKS, GROUPS, 3, OWN, ff), bf16),
            pltpu.VMEM((CHUNKS, 3, 2, OWN, ff), bf16),
            pltpu.VMEM((CHUNKS, 3, OWN, ff), bf16),
            pltpu.VMEM((3, CHUNKS, GROUPS, OWN, ff), bf16),
            pltpu.VMEM((CHUNKS, 2, OWN, ff), f32),
            pltpu.VMEM((2, width, ff), bf16),
            sem((3,)), sem((3,)), sem((3,)), sem((3,)), sem((3,)), sem((3,)), sem((5,)),
        ]
        + [sem((CHUNKS,))] * 8
        + [sem((1,)), sem((CHUNKS, 3, 2)), sem((1,)), sem((CHUNKS, 3, 2))]
        + [sem((3, 2))] * 4,
        compiler_params=pltpu.CompilerParams(
            collective_id=0, has_side_effects=True, vmem_limit_bytes=62 * 2**20
        ),
        cost_estimate=pl.CostEstimate(flops=24 * 10**9, bytes_accessed=14 * 10**6, transcendentals=500000),
    )(tab, tokens, cotangent, w_gate, w_up, w_down)
    return pl.pallas_call(
        publish,
        out_shape=[jax.ShapeDtypeStruct(r.shape, r.dtype) for r in results],
        in_specs=[hbm] * 5,
        out_specs=[hbm] * 5,
        scratch_shapes=[pltpu.VMEM(r.shape, r.dtype) for r in results] + [sem((5,)), sem((5,))],
        compiler_params=pltpu.CompilerParams(vmem_limit_bytes=62 * 2**20),
    )(*results)


def solution(mesh):
    placed = (
        P(("dp", "tensor", "context"), None),
        P(("dp", "tensor", "context"), None),
        P(("dp", "tensor", "context"), None),
        P(("dp", "tensor", "context"), None),
        P(("tensor", "context"), "dp", None),
        P(("tensor", "context"), "dp", None),
        P(("tensor", "context"), None, "dp"),
    )
    return jax.shard_map(
        shards,
        mesh=mesh,
        in_specs=placed,
        out_specs=(
            P(("dp", "tensor", "context"), None),
            P(("dp", "tensor", "context"), None),
            P(("tensor", "context"), "dp", None),
            P(("tensor", "context"), "dp", None),
            P(("tensor", "context"), None, "dp"),
        ),
        check_vma=False,
    )
```
